32 devices in a mesh: teacher: 4 (over y, x), dp: 8 (over z, core).
Axes of the slice: x: 2, y: 2, z: 4, core: 2. Of those that a mesh axis runs over, the one named last changes fastest.
Arguments:
- hid_whisper: bfloat16 [4096, 1280], P(('teacher', 'dp')), may hold values from -6 to 6
- hid_beats: bfloat16 [4096, 768], P(('teacher', 'dp')), may hold values from -6 to 6
- hid_wavlm: bfloat16 [4096, 1024], P(('teacher', 'dp')), may hold values from -6 to 6
- up_whisper: bfloat16 [1280, 5120], P(None, 'teacher'), may hold values from -0.15625 to 0.15625
- down_whisper: bfloat16 [5120, 1280], P('teacher'), may hold values from -0.078125 to 0.078125
- up_beats: bfloat16 [768, 3072], P(None, 'teacher'), may hold values from -0.21875 to 0.21875
- down_beats: bfloat16 [3072, 768], P('teacher'), may hold values from -0.109375 to 0.109375
- up_wavlm: bfloat16 [1024, 4096], P(None, 'teacher'), may hold values from -0.1875 to 0.1875
- down_wavlm: bfloat16 [4096, 1024], P('teacher'), may hold values from -0.09375 to 0.09375
- clip_len: int32 [32], P(('teacher', 'dp')), may hold values from 16 to 128
- send_counts: int32 [4, 8, 8], P('teacher'), may hold values from 0 to 32, as said below
- student_in: bfloat16 [4096, 512], P(('teacher', 'dp')), may hold values from -6 to 6
- w_in: bfloat16 [512, 1536], P('dp'), may hold values from -0.25 to 0.25
- w_out: bfloat16 [1536, 512], P('dp'), may hold values from -0.15625 to 0.15625
- w_head: bfloat16 [512, 3072], P('dp'), may hold values from -0.25 to 0.25
Outputs:
- grad_in: float32 [512, 1536], P('dp')
- grad_out: float32 [1536, 512], P('dp')
- grad_head: float32 [512, 3072], P('dp')
The draws below stay inside these ranges and needn't reach their ends.
Inputs may be any that keep to these rules, and one draw needn't show every extreme that they name: In every group t, each source s hands 128 frames in all (the sum over o of send_counts[t,s,o]), each owner o receives 128 frames in all, and in every group some source hands exactly 32 frames to some owner.
All inputs are finite; a program needn't handle non-finite values.
Results may differ from the reference program's by a relative error of at most 0.0031.
Values may be sent and summed in bfloat16 or wider, within the bound.
No kernel may reach another device: no remote copies, remote signals or barrier semaphores. Data moves between devices by JAX's collectives and lax.ppermute only.
A program may use at most 128 MiB of HBM per device.

```python
import jax
import jax.numpy as jnp
from jax import lax

WH = 1280
HW = 5120
WB = 768
HB = 3072
WL = 1024
HL = 4096
SD = 512
SFF = 1536
FR_DEV = 128
CLIP = 128
CLIPS_DEV = 1
WALL = 3072
FRAMES = 4096
N_TEACHER = 4
N_DP = 8


def draw_send_counts(key, part):
    base = FR_DEV // N_DP
    marked = N_DP // 4

    def one_group(group):
        group_key = jax.random.fold_in(key, group)
        pattern = jnp.concatenate([jnp.full((marked,), base, jnp.int32), jnp.full((marked,), -base, jnp.int32), jnp.zeros((N_DP - 2 * marked,), jnp.int32)])
        pattern = jax.random.permutation(jax.random.fold_in(group_key, 1), pattern)
        owners = jax.random.permutation(jax.random.fold_in(group_key, 2), N_DP).astype(jnp.int32)
        sources = jnp.arange(N_DP, dtype=jnp.int32)
        shifted = (owners[None, :] - sources[:, None]) % N_DP
        return base + pattern[shifted]
    return jax.vmap(one_group)(jnp.arange(N_TEACHER, dtype=jnp.int32))


def touch_ends(values, rng, smallest, largest):
    place = [jax.random.randint(jax.random.fold_in(rng, axis), (), 0, length) for axis, length in enumerate(values.shape)]
    widest = values.shape.index(max(values.shape))
    next_to = place[:widest] + [(place[widest] + 1) % values.shape[widest]] + place[widest + 1:]
    return values.at[tuple(place)].set(smallest).at[tuple(next_to)].set(largest)


def raised(entries, stream_key, source, target, shards_of, factor):
    def block_of(axis_at):
        return (jnp.arange(entries.shape[axis_at]) // (entries.shape[axis_at] // shards_of)).reshape((-1,) + (1,) * (entries.ndim - 1 - axis_at))

    near = jax.random.permutation(stream_key, shards_of)[block_of(target)]
    second = (block_of(target) + shards_of // 2) % shards_of
    return jnp.where((block_of(source) == near) | (block_of(source) == second), factor * entries, entries)


def levels(key, shape, cuts, low, high):
    factor_of, own = 1.0, jax.random.fold_in(key, 6)
    for axis_at, blocks in cuts:
        heights = jnp.exp(jax.random.uniform(jax.random.fold_in(own, axis_at), (blocks,), jnp.float32, low / len(cuts), high / len(cuts)))
        factor_of = factor_of * jnp.repeat(heights, shape[axis_at] // blocks).reshape([-1 if axis == axis_at else 1 for axis in range(len(shape))])
    return factor_of


def bell_draw(rng, extent, width, most, cuts=(), kind=jnp.bfloat16):
    factor_of = levels(rng, extent, cuts, -0.22, 0.18) if cuts else 1.0
    array = jax.random.normal(rng, extent, jnp.float32) * width * factor_of
    return jnp.minimum(jnp.maximum(array, -most), most).astype(kind)


def gaussian_with(own_key, extent, scale, reach, cuts, heavy, kind=jnp.bfloat16):
    result = scale * jax.random.normal(own_key, extent, jnp.float32)
    if cuts:
        result = result * levels(own_key, extent, cuts, -0.22, 0.18)
    return jnp.clip(raised(result, jax.random.fold_in(own_key, 3), *heavy), -reach, reach).astype(kind)


def setup_inputs(seed: int = 0) -> dict:
    keys = jax.random.split(jax.random.key(seed), 16)
    hid_whisper = bell_draw(keys[0], (FRAMES, WH), 1.0, 6.0, ((0, 32),))
    hid_beats = bell_draw(keys[1], (FRAMES, WB), 1.0, 6.0, ((0, 32),))
    hid_wavlm = bell_draw(keys[2], (FRAMES, WL), 1.0, 6.0, ((0, 32),))
    up_whisper = bell_draw(keys[3], (WH, HW), WH ** -0.5, 0.15625, ((1, 4),))
    down_whisper = bell_draw(keys[4], (HW, WH), HW ** -0.5, 0.078125, ((0, 4),))
    up_beats = bell_draw(keys[5], (WB, HB), WB ** -0.5, 0.21875, ((1, 4),))
    down_beats = bell_draw(keys[6], (HB, WB), HB ** -0.5, 0.109375, ((0, 4),))
    up_wavlm = bell_draw(keys[7], (WL, HL), WL ** -0.5, 0.1875, ((1, 4),))
    down_wavlm = bell_draw(keys[8], (HL, WL), HL ** -0.5, 0.09375, ((0, 4),))
    clip_len = touch_ends(jax.random.randint(keys[9], (N_TEACHER * N_DP * CLIPS_DEV,), CLIP // 8, CLIP + 1), jax.random.fold_in(keys[9], 1), CLIP // 8, CLIP).astype(jnp.int32)
    send_counts = draw_send_counts(jax.random.fold_in(keys[15], 71), 0)
    student_in = gaussian_with(keys[11], (FRAMES, SD), 1.0, 6.0, ((0, 32),), (0, 1, 32, 2.75))
    w_in = bell_draw(keys[12], (SD, SFF), SD ** -0.5, 0.25, ((0, 8),))
    w_out = bell_draw(keys[13], (SFF, SD), SFF ** -0.5, 0.15625, ((0, 8),))
    w_head = bell_draw(keys[14], (SD, WALL), SD ** -0.5, 0.25, ((0, 8),))
    return dict(hid_whisper=hid_whisper, hid_beats=hid_beats, hid_wavlm=hid_wavlm, up_whisper=up_whisper, down_whisper=down_whisper, up_beats=up_beats, down_beats=down_beats, up_wavlm=up_wavlm, down_wavlm=down_wavlm, clip_len=clip_len, send_counts=send_counts, student_in=student_in, w_in=w_in, w_out=w_out, w_head=w_head)


EPS = 1e-05

def layer_norm(values):
    wide = values.astype(jnp.float32)
    center = wide - lax.optimization_barrier(jnp.mean(wide, axis=-1, keepdims=True))
    spread = lax.optimization_barrier(jnp.mean(center * center, axis=-1, keepdims=True))
    return center * lax.rsqrt(spread + EPS)

def swoosh_low(pre_act):
    return jax.nn.softplus(pre_act - 4.0) - 0.08 * pre_act - 0.035

def swoosh_slope(pre_act):
    return jax.nn.sigmoid(pre_act - 4.0) - 0.08

def column_scale():
    return jnp.concatenate([jnp.full((WH,), 2.0 / WH, jnp.float32), jnp.full((WB,), 2.0 / WB, jnp.float32), jnp.full((WL,), 2.0 / WL, jnp.float32)])

def reference(hid_whisper, hid_beats, hid_wavlm, up_whisper, down_whisper, up_beats, down_beats, up_wavlm, down_wavlm, clip_len, send_counts, student_in, w_in, w_out, w_head):
    blocks = N_TEACHER * N_DP
    pairs = ((up_whisper, down_whisper), (up_beats, down_beats), (up_wavlm, down_wavlm))

    def teacher_block(inputs):
        pieces = []
        for hidden_in, (up_proj, down_proj) in zip(inputs, pairs):
            normed = layer_norm(hidden_in).astype(jnp.bfloat16)
            quarter = up_proj.shape[1] // N_TEACHER
            total = jnp.zeros(hidden_in.shape, jnp.float32)
            for group in range(N_TEACHER):
                hidden = jax.nn.gelu(jnp.dot(normed, up_proj[:, group * quarter:(group + 1) * quarter], preferred_element_type=jnp.float32), approximate=False).astype(jnp.bfloat16)
                partial_sum = jnp.dot(hidden, down_proj[group * quarter:(group + 1) * quarter, :], preferred_element_type=jnp.float32)
                total = total + partial_sum
            pieces.append(total + hidden_in.astype(jnp.float32))
        return jnp.concatenate(pieces, axis=1).astype(jnp.bfloat16)
    inputs = (hid_whisper.reshape(blocks, FR_DEV, WH), hid_beats.reshape(blocks, FR_DEV, WB), hid_wavlm.reshape(blocks, FR_DEV, WL))
    targets = lax.map(teacher_block, inputs).reshape(blocks * FR_DEV, WH + WB + WL)
    frame_ids = jnp.arange(blocks * FR_DEV, dtype=jnp.int32)
    valid = (frame_ids % CLIP < clip_len[frame_ids // CLIP]).astype(jnp.int32)
    row_start = jnp.cumsum(send_counts, axis=2, dtype=jnp.int32) - send_counts
    col_end = jnp.cumsum(send_counts, axis=1, dtype=jnp.int32)
    col_start = col_end - send_counts
    end_to = jnp.transpose(col_end, (0, 2, 1))
    start_to = jnp.transpose(col_start, (0, 2, 1))
    offset_at = jnp.transpose(row_start, (0, 2, 1))
    positions = jnp.arange(FR_DEV, dtype=jnp.int32)
    source_of = lax.optimization_barrier(jnp.sum((end_to[:, :, None, :] <= positions[None, None, :, None]).astype(jnp.int32), axis=3, dtype=jnp.int32))
    select = jnp.arange(N_DP, dtype=jnp.int32)[None, None, None, :] == source_of[..., None]
    within = positions[None, None, :] - lax.optimization_barrier(jnp.sum(jnp.where(select, start_to[:, :, None, :], 0), axis=3, dtype=jnp.int32))
    offset = lax.optimization_barrier(jnp.sum(jnp.where(select, offset_at[:, :, None, :], 0), axis=3, dtype=jnp.int32))
    group_ids = jnp.arange(N_TEACHER, dtype=jnp.int32)[:, None, None]
    source_row = ((group_ids * N_DP + source_of) * FR_DEV + offset + within).reshape(-1).astype(jnp.int32)
    owner_target = targets[source_row]
    owner_mask = valid[source_row].astype(jnp.float32)
    pre_act = jnp.dot(student_in, w_in, preferred_element_type=jnp.float32)
    activated = swoosh_low(pre_act).astype(jnp.bfloat16)
    features = (student_in.astype(jnp.float32) + jnp.dot(activated, w_out, preferred_element_type=jnp.float32)).astype(jnp.bfloat16)
    predicted = jnp.dot(features, w_head, preferred_element_type=jnp.float32)
    err_grad = ((predicted - owner_target.astype(jnp.float32)) * column_scale()[None, :] * owner_mask[:, None]).astype(jnp.bfloat16)
    grad_head = jnp.dot(features.T, err_grad, preferred_element_type=jnp.float32)
    feat_grad = jnp.dot(err_grad, w_head.T, preferred_element_type=jnp.float32).astype(jnp.bfloat16)
    grad_out = jnp.dot(activated.T, feat_grad, preferred_element_type=jnp.float32)
    act_grad = jnp.dot(feat_grad, w_out.T, preferred_element_type=jnp.float32)
    pre_grad = (act_grad * swoosh_slope(pre_act)).astype(jnp.bfloat16)
    grad_in = jnp.dot(student_in.T, pre_grad, preferred_element_type=jnp.float32)
    return (grad_in, grad_out, grad_head)
```

```python
import jax
import jax.numpy as jnp
from jax import lax
from jax.sharding import PartitionSpec as P

EPS = 1e-05
BF = jnp.bfloat16
F32 = jnp.float32


def layer_norm(values):
    wide = values.astype(jnp.float32)
    center = wide - jnp.mean(wide, axis=-1, keepdims=True)
    spread = jnp.mean(center * center, axis=-1, keepdims=True)
    return center * lax.rsqrt(spread + EPS)


def swoosh_low(pre_act):
    return jax.nn.softplus(pre_act - 4.0) - 0.08 * pre_act - 0.035


def swoosh_slope(pre_act):
    return jax.nn.sigmoid(pre_act - 4.0) - 0.08


def dot(a, b, dims=((1,), (0,))):
    return lax.dot_general(a, b, (dims, ((), ())), preferred_element_type=F32)


def make_body(n_teacher, n_dp):
    n_z = n_dp // 2

    def swap_teacher(k, value):
        return lax.ppermute(value, "teacher", [(t, t ^ k) for t in range(n_teacher)])

    def swap_z(k, value):
        return lax.ppermute(value, "dp", [(d, d ^ (2 * k)) for d in range(n_dp)])

    def swap_core(value):
        return lax.ppermute(value, "dp", [(d, d ^ 1) for d in range(n_dp)])

    def in_order(pieces, index):
        bit = 1
        pieces = list(pieces)
        while bit < len(pieces):
            odd = (index & bit) != 0
            pieces = [jnp.where(odd, pieces[i ^ bit], pieces[i]) for i in range(len(pieces))]
            bit *= 2
        return pieces

    def gather_z(value):
        core = lax.axis_index("dp") % 2
        own = [value] + [swap_z(k, value) for k in range(1, n_z)]
        out = []
        for piece in own:
            other = swap_core(piece)
            out.append(jnp.concatenate(
                [jnp.where(core == 0, piece, other), jnp.where(core == 0, other, piece)], axis=0))
        return out

    def body(hid_whisper, hid_beats, hid_wavlm, up_whisper, down_whisper, up_beats, down_beats,
             up_wavlm, down_wavlm, clip_len, send_counts, student_in, w_in, w_out, w_head):
        t_index = lax.axis_index("teacher")
        d_index = lax.axis_index("dp")
        z_index = d_index // 2
        core = d_index % 2
        frames = hid_whisper.shape[0]
        half = frames // 2
        capacity = 2 * frames // n_dp
        hids = (hid_whisper, hid_beats, hid_wavlm)
        weights = ((up_whisper, down_whisper), (up_beats, down_beats), (up_wavlm, down_wavlm))
        widths = [h.shape[1] for h in hids]
        wall = sum(widths)

        table = send_counts[0]
        col_of = lax.dynamic_index_in_dim(table, d_index, 1, keepdims=False)
        row_of = lax.dynamic_index_in_dim(table, d_index, 0, keepdims=False)
        slots = jnp.arange(capacity, dtype=jnp.int32)
        col_start = jnp.cumsum(col_of, dtype=jnp.int32) - col_of
        packed = student_in[jnp.minimum(col_start[:, None] + slots[None, :], frames - 1)]
        arrived = lax.all_to_all(packed, "dp", split_axis=0, concat_axis=0, tiled=True)
        positions = jnp.arange(frames, dtype=jnp.int32)
        row_end = jnp.cumsum(row_of, dtype=jnp.int32)
        owner_of = jnp.sum((row_end[None, :] <= positions[:, None]).astype(jnp.int32), axis=1, dtype=jnp.int32)
        picked = jnp.arange(n_dp, dtype=jnp.int32)[None, :] == owner_of[:, None]
        within = positions - jnp.sum(jnp.where(picked, (row_end - row_of)[None, :], 0), axis=1, dtype=jnp.int32)
        rows = arrived.reshape(n_dp * capacity, -1)[owner_of * capacity + within]
        clip_slots = frames // clip_len.shape[0]
        lengths = jnp.repeat(clip_len, clip_slots, total_repeat_length=frames)
        valid = (positions % clip_slots < lengths).astype(BF)
        rows = jnp.concatenate([rows, jnp.broadcast_to(valid[:, None], (frames, 128))], axis=1)
        rows = jnp.concatenate([rows] + [swap_teacher(k, rows) for k in range(1, n_teacher)], axis=0)
        s_in, mask = rows[:, :-128], rows[:, -128:-127].astype(F32)

        group = []
        for h in hids:
            from_x, from_y = swap_teacher(1, h), swap_teacher(2, h)
            diag = [swap_teacher(1, from_y[:half]), swap_teacher(2, from_x[half:])]
            group.append(jnp.concatenate([h, from_x, from_y] + diag, axis=0))

        slice_w = wall // n_teacher
        full_in = jnp.concatenate(in_order(gather_z(w_in), z_index), axis=0)
        full_out = jnp.concatenate(in_order(gather_z(w_out), z_index), axis=0)
        head_own = lax.dynamic_slice_in_dim(w_head, t_index * slice_w, slice_w, 1)
        head_own = jnp.concatenate(in_order(gather_z(head_own), z_index), axis=0)
        head_all = [head_own, swap_teacher(1, head_own), swap_teacher(2, head_own), swap_teacher(3, head_own)]
        full_head = jnp.concatenate(in_order(head_all, t_index), axis=1)

        pre_act = dot(s_in, full_in)
        activated = swoosh_low(pre_act).astype(BF)
        features = (s_in.astype(F32) + dot(activated, full_out)).astype(BF)

        first = 0
        head_terms = []
        feat_grad = None
        for h, (up, down), width in zip(group, weights, widths):
            hidden = jax.nn.gelu(dot(layer_norm(h).astype(BF), up), approximate=False).astype(BF)
            partial = dot(hidden, down)
            head_k = lax.slice_in_dim(full_head, first, first + width, axis=1)
            column = first + jnp.arange(width, dtype=jnp.int32)
            mine = (column // slice_w == t_index)[None, :]
            err = jnp.where(mine, dot(features, head_k) - h.astype(F32), 0.0) - partial
            err = (err * (2.0 / width) * mask).astype(BF)
            head_terms.append(dot(features, err, ((0,), (0,))))
            back = dot(err, head_k, ((1,), (1,)))
            feat_grad = back if feat_grad is None else feat_grad + back
            first += width
        feat_grad = feat_grad.astype(BF)
        out_term = dot(activated, feat_grad, ((0,), (0,)))
        act_grad = dot(feat_grad, full_out, ((1,), (1,)))
        pre_grad = (act_grad * swoosh_slope(pre_act)).astype(BF)
        in_term = dot(s_in, pre_grad, ((0,), (0,)))

        def chip_sum(term):
            split = term.reshape(n_z, 2, term.shape[0] // n_dp, term.shape[1])
            keep = lax.dynamic_index_in_dim(split, core, 1, keepdims=False)
            send = lax.dynamic_index_in_dim(split, 1 - core, 1, keepdims=False)
            return keep + swap_core(send.astype(BF)).astype(F32)

        def z_sum(term):
            total = lax.dynamic_index_in_dim(term, z_index, 0, keepdims=False)
            sent = [lax.dynamic_index_in_dim(term, z_index ^ k, 0, keepdims=False).astype(BF) for k in range(1, n_z)]
            for k, value in enumerate(sent):
                total = total + swap_z(k + 1, value).astype(F32)
            return total

        def teacher_sum(term):
            size = term.shape[-1] // n_teacher
            axis = term.ndim - 1
            total = lax.dynamic_slice_in_dim(term, t_index * size, size, axis)
            for k in range(1, n_teacher):
                value = lax.dynamic_slice_in_dim(term, (t_index ^ k) * size, size, axis).astype(BF)
                total = total + swap_teacher(k, value).astype(F32)
            return total

        def teacher_all(value):
            pieces = [value] + [swap_teacher(k, value) for k in range(1, n_teacher)]
            return jnp.concatenate(in_order(pieces, t_index), axis=1)

        grad_head = jnp.concatenate([teacher_all(teacher_sum(z_sum(chip_sum(h)))) for h in head_terms], axis=1)
        grad_out = teacher_all(z_sum(teacher_sum(chip_sum(out_term))))
        grad_in = teacher_all(z_sum(teacher_sum(chip_sum(in_term))))
        return grad_in, grad_out, grad_head

    return body


def solution(mesh):
    in_specs = (
        P(("teacher", "dp"), None),
        P(("teacher", "dp"), None),
        P(("teacher", "dp"), None),
        P(None, "teacher"),
        P("teacher", None),
        P(None, "teacher"),
        P("teacher", None),
        P(None, "teacher"),
        P("teacher", None),
        P(("teacher", "dp")),
        P("teacher", None, None),
        P(("teacher", "dp"), None),
        P("dp", None),
        P("dp", None),
        P("dp", None),
    )
    out_specs = (P("dp", None), P("dp", None), P("dp", None))
    body = make_body(mesh.shape["teacher"], mesh.shape["dp"])
    return jax.shard_map(body, mesh=mesh, in_specs=in_specs, out_specs=out_specs, check_vma=False)
```

```python
import functools

import jax
import jax.numpy as jnp
from jax import lax
from jax.experimental import pallas as pl
from jax.experimental.pallas import tpu as pltpu
from jax.sharding import PartitionSpec as P

EPS = 1e-05
BF = jnp.bfloat16
F32 = jnp.float32
I32 = jnp.int32
BLK = 256
XY_FIRST = 1024
VMEM = pl.BlockSpec(memory_space=pltpu.VMEM)
SMEM = pl.BlockSpec(memory_space=pltpu.SMEM)
ANY = pl.BlockSpec(memory_space=pl.ANY)


def dot(a, b, dims=((1,), (0,))):
    return lax.dot_general(a, b, (dims, ((), ())), preferred_element_type=F32)


def layer_norm(values):
    wide = values.astype(F32)
    center = wide - jnp.mean(wide, axis=-1, keepdims=True)
    spread = jnp.mean(center * center, axis=-1, keepdims=True)
    return center * lax.rsqrt(spread + EPS)


def gelu(x):
    return 0.5 * x * (1.0 + lax.erf(x * 0.7071067811865476))


def aligned(index, size, to):
    return pl.ds(pl.multiple_of(index * size, to), size)


def call(kernel, name, out_shape, in_specs, scratch=(), grid=None, out_specs=None, flops=0, nbytes=0, limit=60):
    many = isinstance(out_shape, (list, tuple))
    if out_specs is None:
        out_specs = [VMEM] * len(out_shape) if many else VMEM
    extra = {} if grid is None else {"grid": grid}
    return pl.pallas_call(
        kernel,
        out_shape=out_shape,
        in_specs=in_specs,
        out_specs=out_specs,
        scratch_shapes=list(scratch),
        name=name,
        cost_estimate=pl.CostEstimate(flops=flops, bytes_accessed=nbytes, transcendentals=0),
        compiler_params=pltpu.CompilerParams(vmem_limit_bytes=limit * 1024 * 1024),
        **extra,
    )


def shape(dims, dtype):
    return jax.ShapeDtypeStruct(dims, dtype)


def pack_kernel(n_dp, cap, table, student, out):
    me = lax.axis_index("dp")
    frames = student.shape[0]
    row = lax.broadcasted_iota(I32, (n_dp * cap, frames), 0)
    col = lax.broadcasted_iota(I32, (n_dp * cap, frames), 1)
    start = jnp.zeros((n_dp * cap, frames), I32)
    running = jnp.int32(0)
    for s in range(n_dp):
        start = jnp.where(row // cap == s, running, start)
        running = running + table[0, s, me]
    pick = (col == start + row % cap).astype(F32).astype(BF)
    out[...] = dot(pick, student[...]).astype(BF)


def unpack_kernel(n_dp, cap, table, clip_len, arrived, out):
    me = lax.axis_index("dp")
    frames, wide = out.shape
    width = arrived.shape[1]
    row = lax.broadcasted_iota(I32, (frames, n_dp * cap), 0)
    col = lax.broadcasted_iota(I32, (frames, n_dp * cap), 1)
    slot = jnp.zeros((frames, n_dp * cap), I32)
    running = jnp.int32(0)
    for o in range(n_dp):
        here = table[0, me, o]
        inside = (row >= running) & (row < running + here)
        slot = jnp.where(inside, o * cap + row - running, slot)
        running = running + here
    pick = (col == slot).astype(F32).astype(BF)
    out[:, :width] = dot(pick, arrived[...]).astype(BF)
    clips = clip_len.shape[0]
    slots = frames // clips
    frame = lax.broadcasted_iota(I32, (frames, wide - width), 0)
    valid = jnp.zeros((frames, wide - width), F32)
    for c in range(clips):
        used = (frame // slots == c) & (frame % slots < clip_len[c])
        valid = jnp.where(used, 1.0, valid)
    out[:, width:] = valid.astype(BF)


def ffn_kernel(first, slice_w, lane0, *refs):
    h_refs, (up, down, out, normed) = refs[:5], refs[5:]
    step = pl.program_id(0)
    width = out.shape[1]
    lanes = pl.ds(lane0, width)

    @pl.when(step == 0)
    def _():
        me = lax.axis_index("teacher")
        at = 0
        for ref in h_refs:
            rows = ref.shape[0]
            h = ref[:, lanes]
            normed[pl.ds(at, rows), :] = layer_norm(h).astype(BF)
            for b in range(0, width, BLK):
                owner = (first + b) // slice_w
                piece = ref[:, pl.ds(lane0 + b, BLK)].astype(F32)
                out[pl.ds(at, rows), pl.ds(b, BLK)] = jnp.where(me == owner, -piece, 0.0)
            at += rows

    hidden = gelu(dot(normed[...], up[...])).astype(BF)
    out[...] -= dot(hidden, down[...])


def ffn(pieces, lane0, first, slice_w, up, down):
    width, hidden = up.shape
    frames = sum(p.shape[0] for p in pieces)
    return call(
        functools.partial(ffn_kernel, first, slice_w, lane0),
        "ffn_%d" % width,
        shape((frames, width), F32),
        [VMEM] * 5
        + [
            pl.BlockSpec((width, BLK), lambda j: (0, j)),
            pl.BlockSpec((BLK, width), lambda j: (j, 0)),
        ],
        scratch=[pltpu.VMEM((frames, width), BF)],
        grid=(hidden // BLK,),
        out_specs=pl.BlockSpec((frames, width), lambda j: (0, 0)),
        flops=4 * frames * width * hidden,
        nbytes=4 * width * hidden,
    )(*pieces, up, down)


def forward_kernel(dims, *refs):
    n_t, n_z, rows, out_rows, widths, slice_w = dims
    s_refs = refs[:n_t]
    w_refs = refs[n_t : n_t + 2 * n_z]
    e_refs = refs[n_t + 2 * n_z : n_t + 2 * n_z + 3]
    act, slope, w_out, err, keep, send = refs[n_t + 2 * n_z + 3 : n_t + 2 * n_z + 9]
    w_in, w_head, feat, feat_t, pred, mask, sem = refs[n_t + 2 * n_z + 9 :]
    step = pl.program_id(0)
    me_t = lax.axis_index("teacher")
    me_d = lax.axis_index("dp")
    z, core = me_d // 2, me_d % 2
    frames = feat.shape[0]
    sd = w_in.shape[0]
    sff = w_in.shape[1]
    parts = out_rows // rows

    @pl.when(step == 0)
    def _():
        copies = []
        for i in range(2 * n_z):
            shard = 2 * (z ^ (i // 2)) + (core if i % 2 == 0 else 1 - core)
            src = w_refs[i]
            copies.append((src.at[:, pl.ds(0, sff)], w_in.at[aligned(shard, rows, 16), :]))
            for p in range(parts):
                copies.append(
                    (
                        src.at[:, pl.ds(sff + p * sd, sd)],
                        w_out.at[pl.ds(pl.multiple_of(shard * out_rows + p * rows, 16), rows), :],
                    )
                )
            copies.append((src.at[:, pl.ds(sff + parts * sd, slice_w)], w_head.at[aligned(shard, rows, 16), :]))
        copies = [pltpu.make_async_copy(a, b, sem.at[i]) for i, (a, b) in enumerate(copies)]
        for c in copies:
            c.start()
        for c in copies:
            c.wait()
        student = jnp.concatenate([r[:, pl.ds(0, sd)] for r in s_refs], axis=0)
        mask[...] = jnp.concatenate([r[:, pl.ds(sd, 128)] for r in s_refs], axis=0).astype(F32)
        total = student.astype(F32)
        for b in range(0, sff, BLK):
            pre = dot(student, w_in[:, pl.ds(b, BLK)])
            low = pre - 4.0
            swoosh = jnp.maximum(low, 0.0) + jnp.log1p(jnp.exp(-jnp.abs(low))) - 0.08 * pre - 0.035
            swoosh = swoosh.astype(BF)
            act[:, pl.ds(b, BLK)] = swoosh
            slope[:, pl.ds(b, BLK)] = 1.0 / (1.0 + jnp.exp(-low)) - 0.08
            total = total + dot(swoosh, w_out[pl.ds(b, BLK), :])
        features = total.astype(BF)
        feat[...] = features
        feat_t[...] = features.T
        pred[...] = dot(features, w_head[...])

    blocks = slice_w // BLK
    at = 0
    for ref, width in zip(e_refs, widths):
        lo, hi = at // BLK, (at + width) // BLK

        @pl.when((step >= lo) & (step < hi))
        def _(ref=ref, width=width):
            value = ref[...]
            mine = step // blocks == me_t
            guess = pred[:, aligned(lax.rem(step, blocks), BLK, BLK)]
            value = value + jnp.where(mine, guess, 0.0)
            scale = (2.0 / width) * mask[...]
            for b in range(0, BLK, 128):
                err[:, pl.ds(b, 128)] = (value[:, b : b + 128] * scale).astype(BF)

        at += width

    product = dot(feat_t[...], err[...])
    for i in range(n_z):
        pair = product[2 * i * rows : 2 * (i + 1) * rows]
        low, high = pair[:rows], pair[rows:]
        keep[i] = jnp.where(core == 0, low, high)
        send[i] = jnp.where(core == 0, high, low).astype(BF)


def forward(s_pieces, w_pieces, e_parts, n_z, rows, out_rows, slice_w, sff):
    n_t = len(s_pieces)
    frames = n_t * s_pieces[0].shape[0]
    sd = s_pieces[0].shape[1] - 128
    widths = [e.shape[1] for e in e_parts]
    wall = sum(widths)
    steps = wall // BLK
    e_specs = []
    at = 0
    for w in widths:
        lo, last = at // BLK, w // BLK - 1
        e_specs.append(pl.BlockSpec((frames, BLK), lambda j, lo=lo, last=last: (0, jnp.clip(j - lo, 0, last))))
        at += w
    whole = lambda dims: pl.BlockSpec(dims, lambda j: (0,) * len(dims))
    return call(
        functools.partial(forward_kernel, (n_t, n_z, rows, out_rows, widths, slice_w)),
        "student_forward",
        [
            shape((frames, sff), BF),
            shape((frames, sff), F32),
            shape((sff, sd), BF),
            shape((frames, wall), BF),
            shape((n_z, rows, wall), F32),
            shape((n_z, rows, wall), BF),
        ],
        [VMEM] * n_t + [ANY] * (2 * n_z) + e_specs,
        out_specs=[
            whole((frames, sff)),
            whole((frames, sff)),
            whole((sff, sd)),
            pl.BlockSpec((frames, BLK), lambda j: (0, j)),
            pl.BlockSpec((n_z, rows, BLK), lambda j: (0, 0, j)),
            pl.BlockSpec((n_z, rows, BLK), lambda j: (0, 0, j)),
        ],
        scratch=[
            pltpu.VMEM((sd, sff), BF),
            pltpu.VMEM((sd, slice_w), BF),
            pltpu.VMEM((frames, sd), BF),
            pltpu.VMEM((sd, frames), BF),
            pltpu.VMEM((frames, slice_w), F32),
            pltpu.VMEM((frames, 128), F32),
            pltpu.SemaphoreType.DMA((2 * n_z * (2 + out_rows // rows),)),
        ],
        grid=(steps,),
        flops=2 * frames * sd * (2 * sff + slice_w + wall),
        nbytes=20 * frames * wall,
    )(*s_pieces, *w_pieces, *e_parts)


def backward_kernel(dims, *refs):
    n_t, n_z, rows, out_rows, slice_w = dims
    s_refs = refs[:n_t]
    h_refs = refs[n_t : 3 * n_t]
    err, act, slope, w_out = refs[3 * n_t : 3 * n_t + 4]
    o_keep, o_send, i_keep, i_send = refs[3 * n_t + 4 : 3 * n_t + 8]
    w_head, student_t, sem = refs[3 * n_t + 8 :]
    me_t = lax.axis_index("teacher")
    me_d = lax.axis_index("dp")
    z, core = me_d // 2, me_d % 2
    copies = []
    for k in range(n_t):
        for c in range(2):
            for i in range(n_z):
                shard = 2 * (z ^ i) + (core if c == 0 else 1 - core)
                copies.append(
                    pltpu.make_async_copy(
                        h_refs[2 * k + c].at[pl.ds(i * rows, rows), :],
                        w_head.at[aligned(shard, rows, 16), aligned(me_t ^ k, slice_w, 128)],
                        sem.at[len(copies)],
                    )
                )
    for c in copies:
        c.start()
    student = jnp.concatenate([r[:, pl.ds(0, w_head.shape[0])] for r in s_refs], axis=0)
    student_t[...] = student.T
    for c in copies:
        c.wait()
    fg = dot(err[...], w_head[...], ((1,), (1,))).astype(BF)
    sff = act.shape[1]
    block = sff // 4
    zs = block // (2 * out_rows)
    for b in range(4):
        part = dot(act[:, pl.ds(b * block, block)].T, fg)
        for i in range(zs):
            low = part[2 * i * out_rows : (2 * i + 1) * out_rows]
            high = part[(2 * i + 1) * out_rows : (2 * i + 2) * out_rows]
            o_keep[b * zs + i] = jnp.where(core == 0, low, high)
            o_send[b * zs + i] = jnp.where(core == 0, high, low).astype(BF)
        back = dot(fg, w_out[pl.ds(b * block, block), :], ((1,), (1,)))
        pre_grad = (back * slope[:, pl.ds(b * block, block)]).astype(BF)
        part = dot(student_t[...], pre_grad)
        for i in range(n_z):
            low = part[2 * i * rows : (2 * i + 1) * rows]
            high = part[(2 * i + 1) * rows : (2 * i + 2) * rows]
            i_keep[i, :, pl.ds(b * block, block)] = jnp.where(core == 0, low, high)
            i_send[i, :, pl.ds(b * block, block)] = jnp.where(core == 0, high, low).astype(BF)


def backward(s_pieces, h_pieces, err, act, slope, w_out, n_z, rows, out_rows, slice_w):
    n_t = len(s_pieces)
    frames, wall = err.shape
    sff, sd = w_out.shape
    return call(
        functools.partial(backward_kernel, (n_t, n_z, rows, out_rows, slice_w)),
        "student_backward",
        [
            shape((n_z, out_rows, sd), F32),
            shape((n_z, out_rows, sd), BF),
            shape((n_z, rows, sff), F32),
            shape((n_z, rows, sff), BF),
        ],
        [VMEM] * n_t + [ANY] * (2 * n_t) + [VMEM] * 4,
        scratch=[
            pltpu.VMEM((sd, wall), BF),
            pltpu.VMEM((sd, frames), BF),
            pltpu.SemaphoreType.DMA((2 * n_t * n_z,)),
        ],
        flops=2 * frames * sd * (wall + 3 * sff),
        nbytes=8 * frames * wall,
    )(*s_pieces, *h_pieces, err, act, slope, w_out)


def head_chip_kernel(n_z, keep, recv, own, *sends):
    z = lax.axis_index("dp") // 2
    wide = own.shape[1]
    lanes = pl.ds(0, wide)
    own[...] = keep[z, :, lanes] + recv[z, :, lanes].astype(F32)
    for k in range(1, n_z):
        at = z ^ k
        sends[k - 1][...] = (keep[at, :, lanes] + recv[at, :, lanes].astype(F32)).astype(BF)


def add_kernel(own, *refs):
    total = own[...]
    for r in refs[:-1]:
        total = total + r[...].astype(F32)
    refs[-1][...] = total.astype(refs[-1].dtype)


def rest_chip_kernel(n_t, dims, ok, orv, ik, irv, hk, hrv, own, *sends):
    sd, sff, wall = dims
    me = lax.axis_index("teacher")
    n_z, rows, _ = ik.shape
    parts = ok.shape[1] // rows
    ow, iw, hw = sd // n_t, sff // n_t, XY_FIRST // n_t
    for k in range(n_t):
        dst = own if k == 0 else sends[k - 1]
        at = me ^ k
        lanes = pl.ds(pl.multiple_of(at * ow, 128), ow)
        for p in range(parts):
            part = pl.ds(p * rows, rows)
            dst[:, :, pl.ds(p * ow, ow)] = (ok[:, part, lanes] + orv[:, part, lanes].astype(F32)).astype(dst.dtype)
        lanes = pl.ds(pl.multiple_of(at * iw, 128), iw)
        dst[:, :, pl.ds(parts * ow, iw)] = (ik[:, :, lanes] + irv[:, :, lanes].astype(F32)).astype(dst.dtype)
        lanes = pl.ds(pl.multiple_of(wall - XY_FIRST + at * hw, 128), hw)
        dst[:, :, pl.ds(parts * ow + iw, hw)] = (hk[:, :, lanes] + hrv[:, :, lanes].astype(F32)).astype(dst.dtype)


def rest_teacher_kernel(n_t, n_z, *refs):
    ins, (own, *sends) = refs[:n_t], refs[n_t:]
    z = lax.axis_index("dp") // 2
    for k in range(n_z):
        at = z ^ k
        total = ins[0][at]
        for r in ins[1:]:
            total = total + r[at].astype(F32)
        dst = own if k == 0 else sends[k - 1]
        dst[...] = total.astype(dst.dtype)


def last_kernel(n_t, dims, *refs):
    sd, sff, wall = dims
    heads, rest, (g_in, g_out, g_head) = refs[:n_t], refs[n_t : 2 * n_t], refs[2 * n_t :]
    me = lax.axis_index("teacher")
    rows = g_in.shape[0]
    parts = g_out.shape[0] // rows
    ow, iw, hw = sd // n_t, sff // n_t, XY_FIRST // n_t
    sums = [h[...].astype(F32) for h in heads]
    while len(sums) > 1:
        sums = [sums[i] + sums[i + 1] for i in range(0, len(sums), 2)]
    g_head[:, : wall - XY_FIRST] = sums[0]
    for k in range(n_t):
        at = me ^ k
        lanes = pl.ds(pl.multiple_of(at * ow, 128), ow)
        for p in range(parts):
            g_out[pl.ds(p * rows, rows), lanes] = rest[k][:, pl.ds(p * ow, ow)]
        g_in[:, pl.ds(pl.multiple_of(at * iw, 128), iw)] = rest[k][:, pl.ds(parts * ow, iw)]
        lanes = pl.ds(pl.multiple_of(wall - XY_FIRST + at * hw, 128), hw)
        g_head[:, lanes] = rest[k][:, pl.ds(parts * ow + iw, hw)]


def make_body(n_t, n_dp):
    n_z = n_dp // 2

    def swap_t(k, value):
        return lax.ppermute(value, "teacher", [(t, t ^ k) for t in range(n_t)])

    def swap_z(k, value):
        return lax.ppermute(value, "dp", [(d, d ^ (2 * k)) for d in range(n_dp)])

    def swap_core(value):
        return lax.ppermute(value, "dp", [(d, d ^ 1) for d in range(n_dp)])

    def body(hid_whisper, hid_beats, hid_wavlm, up_whisper, down_whisper, up_beats, down_beats,
             up_wavlm, down_wavlm, clip_len, send_counts, student_in, w_in, w_out, w_head):
        frames, sd = student_in.shape
        half = frames // 2
        cap = 2 * frames // n_dp
        rows, sff = w_in.shape
        out_rows = w_out.shape[0]
        parts = out_rows // rows
        wall = w_head.shape[1]
        slice_w = wall // n_t
        me_t = lax.axis_index("teacher")
        ww, wb, wl = hid_whisper.shape[1], hid_beats.shape[1], hid_wavlm.shape[1]

        mine = lax.dynamic_slice_in_dim(w_head, me_t * slice_w, slice_w, 1)
        merged = jnp.concatenate(
            [w_in] + [w_out[p * rows : (p + 1) * rows] for p in range(parts)] + [mine], axis=1
        )
        from_z = [merged] + [swap_z(k, merged) for k in range(1, n_z)]
        w_pieces = []
        for piece in from_z:
            w_pieces += [piece, swap_core(piece)]

        def group(value):
            from_x, from_y = swap_t(1, value), swap_t(2, value)
            return [value, from_x, from_y, swap_t(1, from_y[:half]), swap_t(2, from_x[half:])]

        group_a = group(hid_whisper)
        group_b = group(jnp.concatenate([hid_beats, hid_wavlm], axis=1))

        packed = call(
            functools.partial(pack_kernel, n_dp, cap), "pack", shape((n_dp * cap, sd), BF), [SMEM, VMEM]
        )(send_counts, student_in)
        arrived = lax.all_to_all(packed, "dp", split_axis=0, concat_axis=0, tiled=True)
        s_own = call(
            functools.partial(unpack_kernel, n_dp, cap), "unpack", shape((frames, sd + 128), BF), [SMEM, SMEM, VMEM]
        )(send_counts, clip_len, arrived)
        s_pieces = [s_own] + [swap_t(k, s_own) for k in range(1, n_t)]

        heads = jnp.concatenate([p[:, -slice_w:] for p in from_z], axis=0)
        h_pieces = []
        for k in range(n_t):
            piece = heads if k == 0 else swap_t(k, heads)
            h_pieces += [piece, swap_core(piece)]

        e_whisper = ffn(group_a, 0, 0, slice_w, up_whisper, down_whisper)
        e_beats = ffn(group_b, 0, ww, slice_w, up_beats, down_beats)
        e_wavlm = ffn(group_b, wb, ww + wb, slice_w, up_wavlm, down_wavlm)

        act, slope, full_out, err, h_keep, h_send = forward(
            s_pieces, w_pieces, [e_whisper, e_beats, e_wavlm], n_z, rows, out_rows, slice_w, sff
        )
        h_recv = swap_core(h_send)
        head_w = wall - XY_FIRST
        h_own, *h_sends = call(
            functools.partial(head_chip_kernel, n_z), "head_chip",
            [shape((rows, head_w), F32)] + [shape((rows, head_w), BF)] * (n_z - 1), [VMEM] * 2,
        )(h_keep, h_recv)
        h_got = [swap_z(k + 1, v) for k, v in enumerate(h_sends)]
        h_sum = call(add_kernel, "head_z", shape((rows, head_w), BF), [VMEM] * n_z)(h_own, *h_got)
        h_all = [h_sum] + [swap_t(k, h_sum) for k in range(1, n_t)]

        o_keep, o_send, i_keep, i_send = backward(
            s_pieces, h_pieces, err, act, slope, full_out, n_z, rows, out_rows, slice_w
        )
        o_recv, i_recv = swap_core(o_send), swap_core(i_send)
        dims = (sd, sff, wall)
        chunk = (parts * sd + sff + XY_FIRST) // n_t
        r_own, *r_sends = call(
            functools.partial(rest_chip_kernel, n_t, dims), "rest_chip",
            [shape((n_z, rows, chunk), F32)] + [shape((n_z, rows, chunk), BF)] * (n_t - 1), [VMEM] * 6,
        )(o_keep, o_recv, i_keep, i_recv, h_keep, h_recv)
        r_got = [swap_t(k + 1, v) for k, v in enumerate(r_sends)]
        r_own, *r_sends = call(
            functools.partial(rest_teacher_kernel, n_t, n_z), "rest_teacher",
            [shape((rows, chunk), F32)] + [shape((rows, chunk), BF)] * (n_z - 1), [VMEM] * n_t,
        )(r_own, *r_got)
        r_got = [swap_z(k + 1, v) for k, v in enumerate(r_sends)]
        r_sum = call(add_kernel, "rest_z", shape((rows, chunk), F32), [VMEM] * n_z)(r_own, *r_got)
        r_all = [r_sum] + [swap_t(k, r_sum) for k in range(1, n_t)]

        grad_in, grad_out, grad_head = call(
            functools.partial(last_kernel, n_t, dims), "last",
            [shape((rows, sff), F32), shape((out_rows, sd), F32), shape((rows, wall), F32)], [VMEM] * (2 * n_t),
        )(*h_all, *r_all)
        return grad_in, grad_out, grad_head

    return body


def solution(mesh):
    rows = P(("teacher", "dp"), None)
    in_specs = (
        rows, rows, rows,
        P(None, "teacher"), P("teacher", None),
        P(None, "teacher"), P("teacher", None),
        P(None, "teacher"), P("teacher", None),
        P(("teacher", "dp")), P("teacher", None, None), rows,
        P("dp", None), P("dp", None), P("dp", None),
    )
    out_specs = (P("dp", None), P("dp", None), P("dp", None))
    body = make_body(mesh.shape["teacher"], mesh.shape["dp"])
    return jax.shard_map(body, mesh=mesh, in_specs=in_specs, out_specs=out_specs, check_vma=False)
```

```python
import functools

import jax
import jax.numpy as jnp
from jax import lax
from jax.experimental import pallas as pl
from jax.experimental.pallas import tpu as pltpu
from jax.sharding import PartitionSpec as P

EPS = 1e-05
BF = jnp.bfloat16
F32 = jnp.float32
I32 = jnp.int32
BLK = 256
FFN_MB = 50
VMEM = pl.BlockSpec(memory_space=pltpu.VMEM)
SMEM = pl.BlockSpec(memory_space=pltpu.SMEM)
ANY = pl.BlockSpec(memory_space=pl.ANY)
HBM = pl.BlockSpec(memory_space=pltpu.HBM)


def dot(a, b, dims=((1,), (0,))):
    return lax.dot_general(a, b, (dims, ((), ())), preferred_element_type=F32)


def layer_norm(values):
    wide = values.astype(F32)
    center = wide - jnp.mean(wide, axis=-1, keepdims=True)
    spread = jnp.mean(center * center, axis=-1, keepdims=True)
    return center * lax.rsqrt(spread + EPS)


def gelu(x):
    return 0.5 * x * (1.0 + lax.erf(x * 0.7071067811865476))


def aligned(index, size, to):
    return pl.ds(pl.multiple_of(index * size, to), size)


def call(kernel, name, out_shape, in_specs, scratch=(), out_specs=None, limit=8, us=1):
    many = isinstance(out_shape, (list, tuple))
    if out_specs is None:
        out_specs = [VMEM] * len(out_shape) if many else VMEM
    return pl.pallas_call(
        kernel,
        out_shape=out_shape,
        in_specs=in_specs,
        out_specs=out_specs,
        scratch_shapes=list(scratch),
        name=name,
        cost_estimate=pl.CostEstimate(flops=int(us * 1e9), bytes_accessed=int(us * 3e6), transcendentals=0),
        compiler_params=pltpu.CompilerParams(vmem_limit_bytes=limit * 1024 * 1024),
    )


def shape(dims, dtype):
    return jax.ShapeDtypeStruct(dims, dtype)


def pack_kernel(n_t, n_dp, cap, table, student, w_head, out):
    me = lax.axis_index("dp")
    frames, sd = student.shape
    rows = 2 * cap
    row = lax.broadcasted_iota(I32, (n_dp * rows, frames), 0)
    col = lax.broadcasted_iota(I32, (n_dp * rows, frames), 1)
    start = jnp.zeros((n_dp * rows, frames), I32)
    running = jnp.int32(0)
    for s in range(n_dp):
        start = jnp.where(row // rows == s, running, start)
        running = running + table[0, s, me]
    pick = (col == start + row % cap).astype(F32).astype(BF)
    half = sd // 2
    left, right = dot(pick, student[:, :half]), dot(pick, student[:, half:])
    first = lax.broadcasted_iota(I32, left.shape, 0) % rows < cap
    out[:, :half] = jnp.where(first, left, right).astype(BF)
    slice_w = w_head.shape[1] // n_t
    mine = w_head[:, aligned(lax.axis_index("teacher"), slice_w, 128)]
    for d in range(n_dp):
        lane = d % 2 * (slice_w // 2)
        out[pl.ds(d * rows, rows), half:] = mine[:, lane : lane + slice_w // 2]


def unpack_kernel(n_dp, cap, table, clip_len, arrived, out, head):
    me = lax.axis_index("dp")
    copies, frames, wide = out.shape
    sd = wide - 128
    half = sd // 2
    rows = 2 * cap
    row = lax.broadcasted_iota(I32, (frames, n_dp * rows), 0)
    col = lax.broadcasted_iota(I32, (frames, n_dp * rows), 1)
    slot = jnp.zeros((frames, n_dp * rows), I32)
    running = jnp.int32(0)
    for o in range(n_dp):
        here = table[0, me, o]
        inside = (row >= running) & (row < running + here)
        slot = jnp.where(inside, o * rows + row - running, slot)
        running = running + here
    parts = [
        dot((col == slot + at).astype(F32).astype(BF), arrived[:, :half]).astype(BF) for at in (0, cap)
    ]
    clips = clip_len.shape[0]
    slots = frames // clips
    frame = lax.broadcasted_iota(I32, (frames, wide - sd), 0)
    valid = jnp.zeros((frames, wide - sd), F32)
    for c in range(clips):
        used = (frame // slots == c) & (frame % slots < clip_len[c])
        valid = jnp.where(used, 1.0, valid)
    for k in range(copies):
        out[k, :, :half] = parts[0]
        out[k, :, half:sd] = parts[1]
        out[k, :, sd:] = valid.astype(BF)
    head[...] = arrived[:, half:]


def copy_all(pairs, sem):
    copies = [pltpu.make_async_copy(a, b, sem.at[i]) for i, (a, b) in enumerate(pairs)]
    for c in copies:
        c.start()
    for c in copies:
        c.wait()


def merge_kernel(w_in, w_out, whisper, beats, wavlm, after, merged, hid, sem):
    rows, sff = w_in.shape
    sd = w_out.shape[1]
    pairs = [(w_in, merged.at[:, pl.ds(0, sff)])]
    for p in range(w_out.shape[0] // rows):
        pairs.append((w_out.at[pl.ds(p * rows, rows), :], merged.at[:, pl.ds(sff + p * sd, sd)]))
    at = 0
    for ref in (whisper, beats, wavlm):
        pairs.append((ref, hid.at[:, pl.ds(at, ref.shape[1])]))
        at += ref.shape[1]
    copy_all(pairs, sem)


def halves_kernel(from_x, from_y, to_y, to_x, sem):
    half = to_x.shape[0]
    copy_all([(from_x.at[pl.ds(half, half), :], to_y), (from_y.at[pl.ds(0, half), :], to_x)], sem)


def ffn_kernel(slice_w, n, *refs):
    h_refs, w_refs, after, e_refs = refs[:n], refs[n : n + 6], refs[n + 6], refs[n + 7 : n + 10]
    hid, w_bufs, e_bufs, normed, sem = refs[n + 10], refs[n + 11 : n + 17], e_refs, refs[n + 17], refs[n + 18]
    me = lax.axis_index("teacher")
    frames = hid.shape[0]
    half = frames // 2
    pairs = []
    at = 0
    for ref in h_refs:
        pairs.append((ref, hid.at[pl.ds(at, ref.shape[0]), :]))
        at += ref.shape[0]
    pairs += list(zip(w_refs, w_bufs))
    copies = [pltpu.make_async_copy(a, b, sem.at[i]) for i, (a, b) in enumerate(pairs)]
    for c in copies:
        c.start()
    for c in copies[:n]:
        c.wait()
    starts = []
    first = 0
    for e in e_bufs:
        starts.append(first)
        first += e.shape[1]
    for k in (0, 2, 1):
        up, down, e = w_bufs[2 * k], w_bufs[2 * k + 1], e_bufs[k]
        width = e.shape[1]
        normed[:, pl.ds(0, width)] = layer_norm(hid[:, pl.ds(starts[k], width)]).astype(BF)
        copies[n + 2 * k].wait()
        hidden = [gelu(dot(normed[pl.ds(r, half), pl.ds(0, width)], up[...])).astype(BF) for r in (0, half)]
        copies[n + 2 * k + 1].wait()
        for i, r in enumerate((0, half)):
            e[pl.ds(r, half), :] = -dot(hidden[i], down[...])
        for b in range(0, width, BLK):

            @pl.when(me == (starts[k] + b) // slice_w)
            def _(b=b, e=e, k=k):
                e[:, pl.ds(b, BLK)] -= hid[:, pl.ds(starts[k] + b, BLK)].astype(F32)


def ffn(pieces, weights, slice_w, after):
    frames = sum(p.shape[0] for p in pieces)
    wall = pieces[0].shape[1]
    widths = [w.shape[1] for w in weights[1::2]]
    n = len(pieces)
    return call(
        functools.partial(ffn_kernel, slice_w, n),
        "ffn",
        [shape((frames, w), F32) for w in widths],
        [HBM] * (n + 6) + [ANY],
        scratch=[pltpu.VMEM((frames, wall), BF)]
        + [pltpu.VMEM(w.shape, BF) for w in weights]
        + [pltpu.VMEM((frames, max(widths)), BF), pltpu.SemaphoreType.DMA((n + 6,))],
        limit=FFN_MB,
        us=13,
    )(*pieces, *weights, after)


def forward_kernel(dims, *refs):
    n_t, n_z, rows, out_rows, slice_w = dims
    s_ref, w_refs, h_refs, refs = refs[0], refs[1 : 1 + 2 * n_z], refs[1 + 2 * n_z : 3 + 2 * n_z], refs[3 + 2 * n_z + n_t - 1 :]
    e_refs, (act, slope, w_out, err, keep, send), (w_in, w_head, pred, sem) = refs[:3], refs[3:9], refs[9:]
    me_t = lax.axis_index("teacher")
    me_d = lax.axis_index("dp")
    z, core = me_d // 2, me_d % 2
    sd, sff = w_in.shape
    parts = out_rows // rows
    pairs = []
    for i in range(2 * n_z):
        shard = 2 * (z ^ (i // 2)) + (core if i % 2 == 0 else 1 - core)
        src = w_refs[i]
        pairs.append((src.at[:, pl.ds(0, sff)], w_in.at[aligned(shard, rows, 16), :]))
        for p in range(parts):
            at = pl.multiple_of(shard * out_rows + p * rows, 16)
            pairs.append((src.at[:, pl.ds(sff + p * sd, sd)], w_out.at[pl.ds(at, rows), :]))
    for c in range(2):
        pairs.append((h_refs[c], w_head.at[:, aligned(core if c == 0 else 1 - core, slice_w // 2, 128)]))
    copy_all(pairs, sem)
    order = [me_t ^ k for k in range(n_t)]
    student = jnp.concatenate([s_ref[k, :, pl.ds(0, sd)] for k in order], axis=0)
    mask = jnp.concatenate([s_ref[k, :, pl.ds(sd, 128)] for k in order], axis=0).astype(F32)
    total = student.astype(F32)
    for b in range(0, sff, BLK):
        pre = dot(student, w_in[:, pl.ds(b, BLK)])
        low = pre - 4.0
        small = jnp.exp(-jnp.abs(low))
        swoosh = jnp.maximum(low, 0.0) + jnp.log(1.0 + small) - 0.08 * pre - 0.035
        swoosh = swoosh.astype(BF)
        act[:, pl.ds(b, BLK)] = swoosh
        slope[:, pl.ds(b, BLK)] = jnp.where(low >= 0.0, 1.0, small) / (1.0 + small) - 0.08
        total = total + dot(swoosh, w_out[pl.ds(b, BLK), :])
    features = total.astype(BF)
    feat_t = features.T
    pred[...] = dot(features, w_head[...])

    at = 0
    for ref in e_refs:
        width = ref.shape[1]
        scale = (2.0 / width) * mask
        for b in range(0, width, BLK):
            col = at + b
            value = ref[:, pl.ds(b, BLK)]
            guess = pred[:, pl.ds(col % slice_w, BLK)]
            value = value + jnp.where(me_t == col // slice_w, guess, 0.0)
            value = jnp.concatenate([value[:, c : c + 128] * scale for c in range(0, BLK, 128)], axis=1).astype(BF)
            err[:, pl.ds(col, BLK)] = value
            product = dot(feat_t, value)
            for i in range(n_z):
                pair = product[2 * i * rows : 2 * (i + 1) * rows]
                low, high = pair[:rows], pair[rows:]
                keep[i, :, pl.ds(col, BLK)] = jnp.where(core == 0, low, high)
                send[i, :, pl.ds(col, BLK)] = jnp.where(core == 0, high, low).astype(BF)
        at += width


def forward(s_all, w_pieces, h_pieces, after, e_parts, n_z, rows, out_rows, slice_w, sff):
    n_t, frames, sd = s_all.shape
    frames, sd = n_t * frames, sd - 128
    wall = sum(e.shape[1] for e in e_parts)
    return call(
        functools.partial(forward_kernel, (n_t, n_z, rows, out_rows, slice_w)),
        "student_forward",
        [
            shape((frames, sff), BF),
            shape((frames, sff), F32),
            shape((sff, sd), BF),
            shape((frames, wall), BF),
            shape((n_z, rows, wall), F32),
            shape((n_z, rows, wall), BF),
        ],
        [VMEM] + [ANY] * (2 * n_z + 2 + n_t - 1) + [VMEM] * 3,
        scratch=[
            pltpu.VMEM((sd, sff), BF),
            pltpu.VMEM((sd, slice_w), BF),
            pltpu.VMEM((frames, slice_w), F32),
        ]
        + [pltpu.SemaphoreType.DMA((2 * n_z * (1 + out_rows // rows) + 2,))],
        limit=16,
        us=7,
    )(s_all, *w_pieces, *h_pieces, *after, *e_parts)


def backward_kernel(dims, *refs):
    n_t, n_z, rows, out_rows, slice_w = dims
    s_ref, h_refs = refs[0], refs[1 : 1 + 2 * n_t]
    err, act, slope, w_out, after, keep, send, w_head, student_t, sem = refs[1 + 2 * n_t :]
    me_t = lax.axis_index("teacher")
    me_d = lax.axis_index("dp")
    z, core = me_d // 2, me_d % 2
    copies = []
    for k in range(n_t):
        for c in range(2):
            at = (me_t ^ k) * slice_w + (core if c == 0 else 1 - core) * (slice_w // 2)
            dst = w_head.at[:, pl.ds(pl.multiple_of(at, 128), slice_w // 2)]
            copies.append(pltpu.make_async_copy(h_refs[2 * k + c], dst, sem.at[len(copies)]))
    for c in copies:
        c.start()
    sd = w_head.shape[0]
    student = jnp.concatenate([s_ref[me_t ^ k, :, pl.ds(0, sd)] for k in range(n_t)], axis=0)
    student_t[...] = student.T
    for c in copies:
        c.wait()
    fg = dot(err[...], w_head[...], ((1,), (1,))).astype(BF)
    sff = act.shape[1]
    block = sff // 4
    zs = block // (2 * out_rows)
    for b in range(4):
        part = dot(act[:, pl.ds(b * block, block)].T, fg)
        for i in range(zs):
            for p in range(out_rows // rows):
                at = 2 * i * out_rows + p * rows
                low, high = part[at : at + rows], part[at + out_rows : at + out_rows + rows]
                lanes = pl.ds(p * sd, sd)
                keep[b * zs + i, :, lanes] = jnp.where(core == 0, low, high)
                send[b * zs + i, :, lanes] = jnp.where(core == 0, high, low).astype(BF)
        back = dot(fg, w_out[pl.ds(b * block, block), :], ((1,), (1,)))
        pre_grad = (back * slope[:, pl.ds(b * block, block)]).astype(BF)
        part = dot(student_t[...], pre_grad)
        for i in range(n_z):
            low = part[2 * i * rows : (2 * i + 1) * rows]
            high = part[(2 * i + 1) * rows : (2 * i + 2) * rows]
            lanes = pl.ds(out_rows // rows * sd + b * block, block)
            keep[i, :, lanes] = jnp.where(core == 0, low, high)
            send[i, :, lanes] = jnp.where(core == 0, high, low).astype(BF)


def backward(s_all, h_pieces, err, act, slope, w_out, after, n_z, rows, out_rows, slice_w):
    n_t = s_all.shape[0]
    frames, wall = err.shape
    sff, sd = w_out.shape
    wide = out_rows // rows * sd + sff
    return call(
        functools.partial(backward_kernel, (n_t, n_z, rows, out_rows, slice_w)),
        "student_backward",
        [shape((n_z, rows, wide), F32), shape((n_z, rows, wide), BF)],
        [VMEM] + [ANY] * (2 * n_t) + [VMEM] * 4 + [ANY],
        scratch=[
            pltpu.VMEM((sd, wall), BF),
            pltpu.VMEM((sd, frames), BF),
            pltpu.SemaphoreType.DMA((2 * n_t,)),
        ],
        limit=16,
        us=6,
    )(s_all, *h_pieces, err, act, slope, w_out, after)


def add_kernel(own, *refs):
    total = own[...]
    for r in refs[:-1]:
        total = total + r[...].astype(F32)
    refs[-1][...] = total.astype(refs[-1].dtype)


def chip_kernel(n_t, splits, keep, recv, *outs):
    me = lax.axis_index("teacher")
    own, sends = outs[0], outs[1:]
    at = 0
    for first, width in splits:
        w = width // n_t
        for k in range(n_t):
            t = me ^ k if len(sends) > 1 else k
            lanes = pl.ds(pl.multiple_of(first + t * w, 128), w)
            value = keep[:, :, lanes] + recv[:, :, lanes].astype(F32)
            if len(sends) > 1:
                dst = own if k == 0 else sends[k - 1]
                dst[:, :, pl.ds(at, w)] = value.astype(dst.dtype)
            else:
                sends[0][k, :, :, pl.ds(at, w)] = value.astype(BF)

                @pl.when(me == k)
                def _(value=value, at=at, w=w):
                    own[:, :, pl.ds(at, w)] = value

        at += w


def teacher_kernel(n_t, n_z, mine, *refs):
    got, own, sends = refs[: -n_z], refs[-n_z], refs[len(refs) - n_z + 1 :]
    z = lax.axis_index("dp") // 2
    me = lax.axis_index("teacher")
    for k in range(n_z):
        at = z ^ k
        total = mine[at]
        for j in range(1, n_t):
            value = got[0][me ^ j, at] if len(got) == 1 else got[j - 1][at]
            total = total + value.astype(F32)
        dst = own if k == 0 else sends[k - 1]
        dst[...] = total.astype(dst.dtype)


def last_kernel(n_t, *refs):
    heads, rest, (g_in, g_out, g_head) = refs[:n_t], refs[n_t : 2 * n_t], refs[2 * n_t :]
    me = lax.axis_index("teacher")
    rows = g_in.shape[0]
    parts = g_out.shape[0] // rows
    ow, iw, hw = g_out.shape[1] // n_t, g_in.shape[1] // n_t, g_head.shape[1] // n_t
    for k in range(n_t):
        at = me ^ k
        g_head[:, aligned(at, hw, 128)] = heads[k][...]
        for p in range(parts):
            g_out[pl.ds(p * rows, rows), aligned(at, ow, 128)] = rest[k][:, pl.ds(p * ow, ow)]
        g_in[:, aligned(at, iw, 128)] = rest[k][:, pl.ds(parts * ow, iw)]


def make_body(n_t, n_dp):
    n_z = n_dp // 2

    def swap_t(k, value):
        return lax.ppermute(value, "teacher", [(t, t ^ k) for t in range(n_t)])

    def swap_z(k, value):
        return lax.ppermute(value, "dp", [(d, d ^ (2 * k)) for d in range(n_dp)])

    def swap_core(value):
        return lax.ppermute(value, "dp", [(d, d ^ 1) for d in range(n_dp)])

    def body(hid_whisper, hid_beats, hid_wavlm, up_whisper, down_whisper, up_beats, down_beats,
             up_wavlm, down_wavlm, clip_len, send_counts, student_in, w_in, w_out, w_head):
        frames, sd = student_in.shape
        half = frames // 2
        cap = 2 * frames // n_dp
        rows, sff = w_in.shape
        out_rows = w_out.shape[0]
        parts = out_rows // rows
        wall = w_head.shape[1]
        slice_w = wall // n_t
        packed = call(
            functools.partial(pack_kernel, n_t, n_dp, cap), "pack",
            shape((n_dp * rows, (sd + slice_w) // 2), BF), [SMEM, VMEM, VMEM], limit=60,
        )(send_counts, student_in, w_head)
        arrived = lax.all_to_all(packed, "dp", split_axis=0, concat_axis=0, tiled=True)

        merged, hid = call(
            merge_kernel, "merge", [shape((rows, sff + parts * sd), BF), shape((frames, wall), BF)],
            [HBM] * 5 + [ANY], scratch=[pltpu.SemaphoreType.DMA((parts + 4,))], limit=60,
        )(w_in, w_out, hid_whisper, hid_beats, hid_wavlm, packed)
        from_z = [merged] + [swap_z(k, merged) for k in range(1, n_z)]

        from_x, from_y = swap_t(1, hid), swap_t(2, hid)
        to_y, to_x = call(
            halves_kernel, "halves", [shape((half, wall), BF)] * 2, [HBM] * 2,
            scratch=[pltpu.SemaphoreType.DMA((2,))], limit=60,
        )(from_x, from_y)
        group = [hid, from_x, from_y, swap_t(1, to_x), swap_t(2, to_y)]

        s_own, head = call(
            functools.partial(unpack_kernel, n_dp, cap), "unpack",
            [shape((n_t, frames, sd + 128), BF), shape((sd, slice_w // 2), BF)], [SMEM, SMEM, VMEM], limit=60,
        )(send_counts, clip_len, arrived)
        s_all = lax.all_to_all(s_own, "teacher", split_axis=0, concat_axis=0, tiled=True)
        h_mine = [head] + [swap_t(k, head) for k in range(1, n_t)]
        e_parts = ffn(group, (up_whisper, down_whisper, up_beats, down_beats, up_wavlm, down_wavlm), slice_w, s_own)
        from_z, h_mine, _ = lax.optimization_barrier((from_z, h_mine, e_parts[0]))
        w_pieces, h_pieces = [], []
        for piece in from_z:
            w_pieces += [piece, swap_core(piece)]
        for piece in h_mine:
            h_pieces += [piece, swap_core(piece)]

        act, slope, full_out, err, h_keep, h_send = forward(
            s_all, w_pieces, h_pieces[:2], h_mine[1:], e_parts, n_z, rows, out_rows, slice_w, sff
        )
        def chip_sum(keep, send, splits, many):
            chunk = keep.shape[2] // n_t
            sends = [shape((n_z, rows, chunk), BF)] * (n_t - 1) if many else [shape((n_t, n_z, rows, chunk), BF)]
            return call(
                functools.partial(chip_kernel, n_t, splits), "chip",
                [shape((n_z, rows, chunk), F32)] + sends, [VMEM] * 2,
            )(keep, swap_core(send))

        def z_sum(mine, got):
            chunk = mine.shape[2]
            own, *sends = call(
                functools.partial(teacher_kernel, n_t, n_z), "over_teacher",
                [shape((rows, chunk), F32)] + [shape((rows, chunk), BF)] * (n_z - 1), [VMEM] * (1 + len(got)),
            )(mine, *got)
            got = [swap_z(k + 1, v) for k, v in enumerate(sends)]
            total = call(add_kernel, "over_z", shape((rows, chunk), F32), [VMEM] * n_z)(own, *got)
            return [total] + [swap_t(k, total) for k in range(1, n_t)]

        h_own, h_out = chip_sum(h_keep, h_send, [(0, wall)], False)
        h_got = lax.all_to_all(h_out, "teacher", split_axis=0, concat_axis=0, tiled=True)
        keep, send = backward(s_all, h_pieces, err, act, slope, full_out, h_own, n_z, rows, out_rows, slice_w)
        splits = [(p * sd, sd) for p in range(parts)] + [(parts * sd, sff)]
        r_own, *r_sends = chip_sum(keep, send, splits, True)
        r_got = [swap_t(k + 1, v) for k, v in enumerate(r_sends)]
        h_all = z_sum(h_own, [h_got])
        r_all = z_sum(r_own, r_got)
        grad_in, grad_out, grad_head = call(
            functools.partial(last_kernel, n_t), "last",
            [shape((rows, sff), F32), shape((out_rows, sd), F32), shape((rows, wall), F32)], [VMEM] * (2 * n_t),
        )(*h_all, *r_all)
        return grad_in, grad_out, grad_head

    return body


def solution(mesh):
    rows = P(("teacher", "dp"), None)
    in_specs = (
        rows, rows, rows,
        P(None, "teacher"), P("teacher", None),
        P(None, "teacher"), P("teacher", None),
        P(None, "teacher"), P("teacher", None),
        P(("teacher", "dp")), P("teacher", None, None), rows,
        P("dp", None), P("dp", None), P("dp", None),
    )
    out_specs = (P("dp", None), P("dp", None), P("dp", None))
    body = make_body(mesh.shape["teacher"], mesh.shape["dp"])
    return jax.shard_map(body, mesh=mesh, in_specs=in_specs, out_specs=out_specs, check_vma=False)
```

```python
import functools

import jax
import jax.numpy as jnp
from jax import lax
from jax.experimental import pallas as pl
from jax.experimental.pallas import tpu as pltpu
from jax.sharding import PartitionSpec as P

EPS = 1e-05
BF = jnp.bfloat16
F32 = jnp.float32
I32 = jnp.int32
BLK = 256
FFN_MB = 50
STUDENT_MB = 44
VMEM = pl.BlockSpec(memory_space=pltpu.VMEM)
SMEM = pl.BlockSpec(memory_space=pltpu.SMEM)
ANY = pl.BlockSpec(memory_space=pl.ANY)
HBM = pl.BlockSpec(memory_space=pltpu.HBM)


def dot(a, b, dims=((1,), (0,))):
    return lax.dot_general(a, b, (dims, ((), ())), preferred_element_type=F32)


def layer_norm(values):
    wide = values.astype(F32)
    center = wide - jnp.mean(wide, axis=-1, keepdims=True)
    spread = jnp.mean(center * center, axis=-1, keepdims=True)
    return center * lax.rsqrt(spread + EPS)


def gelu(x):
    return 0.5 * x * (1.0 + lax.erf(x * 0.7071067811865476))


def aligned(index, size, to):
    return pl.ds(pl.multiple_of(index * size, to), size)


def call(kernel, name, out_shape, in_specs, scratch=(), out_specs=None, limit=8, us=1):
    many = isinstance(out_shape, (list, tuple))
    if out_specs is None:
        out_specs = [VMEM] * len(out_shape) if many else VMEM
    return pl.pallas_call(
        kernel,
        out_shape=out_shape,
        in_specs=in_specs,
        out_specs=out_specs,
        scratch_shapes=list(scratch),
        name=name,
        cost_estimate=pl.CostEstimate(flops=int(us * 1e9), bytes_accessed=int(us * 3e6), transcendentals=0),
        compiler_params=pltpu.CompilerParams(vmem_limit_bytes=limit * 1024 * 1024),
    )


def shape(dims, dtype):
    return jax.ShapeDtypeStruct(dims, dtype)


def pack_kernel(n_t, n_dp, cap, table, student, w_head, out):
    me = lax.axis_index("dp")
    frames, sd = student.shape
    rows = 2 * cap
    row = lax.broadcasted_iota(I32, (n_dp * rows, frames), 0)
    col = lax.broadcasted_iota(I32, (n_dp * rows, frames), 1)
    start = jnp.zeros((n_dp * rows, frames), I32)
    running = jnp.int32(0)
    for s in range(n_dp):
        start = jnp.where(row // rows == s, running, start)
        running = running + table[0, s, me]
    pick = (col == start + row % cap).astype(F32).astype(BF)
    half = sd // 2
    left, right = dot(pick, student[:, :half]), dot(pick, student[:, half:])
    first = lax.broadcasted_iota(I32, left.shape, 0) % rows < cap
    out[:, :half] = jnp.where(first, left, right).astype(BF)
    slice_w = w_head.shape[1] // n_t
    mine = w_head[:, aligned(lax.axis_index("teacher"), slice_w, 128)]
    for d in range(n_dp):
        lane = d % 2 * (slice_w // 2)
        out[pl.ds(d * rows, rows), half:] = mine[:, lane : lane + slice_w // 2]


def unpack_kernel(n_dp, cap, table, clip_len, arrived, out, head):
    me = lax.axis_index("dp")
    copies, frames, wide = out.shape
    sd = wide - 128
    half = sd // 2
    rows = 2 * cap
    row = lax.broadcasted_iota(I32, (frames, n_dp * rows), 0)
    col = lax.broadcasted_iota(I32, (frames, n_dp * rows), 1)
    slot = jnp.zeros((frames, n_dp * rows), I32)
    running = jnp.int32(0)
    for o in range(n_dp):
        here = table[0, me, o]
        inside = (row >= running) & (row < running + here)
        slot = jnp.where(inside, o * rows + row - running, slot)
        running = running + here
    parts = [
        dot((col == slot + at).astype(F32).astype(BF), arrived[:, :half]).astype(BF) for at in (0, cap)
    ]
    clips = clip_len.shape[0]
    slots = frames // clips
    frame = lax.broadcasted_iota(I32, (frames, wide - sd), 0)
    valid = jnp.zeros((frames, wide - sd), F32)
    for c in range(clips):
        used = (frame // slots == c) & (frame % slots < clip_len[c])
        valid = jnp.where(used, 1.0, valid)
    for k in range(copies):
        out[k, :, :half] = parts[0]
        out[k, :, half:sd] = parts[1]
        out[k, :, sd:] = valid.astype(BF)
    head[...] = arrived[:, half:]


def copy_all(pairs, sem):
    copies = [pltpu.make_async_copy(a, b, sem.at[i]) for i, (a, b) in enumerate(pairs)]
    for c in copies:
        c.start()
    for c in copies:
        c.wait()


def merge_kernel(w_in, w_out, whisper, beats, wavlm, after, merged, hid, sem):
    rows, sff = w_in.shape
    sd = w_out.shape[1]
    pairs = [(w_in, merged.at[:, pl.ds(0, sff)])]
    for p in range(w_out.shape[0] // rows):
        pairs.append((w_out.at[pl.ds(p * rows, rows), :], merged.at[:, pl.ds(sff + p * sd, sd)]))
    at = 0
    for ref in (whisper, beats, wavlm):
        pairs.append((ref, hid.at[:, pl.ds(at, ref.shape[1])]))
        at += ref.shape[1]
    copy_all(pairs, sem)


def halves_kernel(from_x, from_y, *refs):
    to_y, to_x, sem = refs[-3:]
    half = to_x.shape[0]
    copy_all([(from_x.at[pl.ds(half, half), :], to_y), (from_y.at[pl.ds(0, half), :], to_x)], sem)


def ffn_kernel(slice_w, n, *refs):
    h_refs, w_refs, refs = refs[:n], refs[n : n + 6], refs[-12:]
    e_bufs, hid, w_bufs, (normed, sem) = refs[:3], refs[3], refs[4:10], refs[10:]
    me = lax.axis_index("teacher")
    frames = hid.shape[0]
    half = frames // 2
    pairs = []
    at = 0
    for ref in h_refs:
        pairs.append((ref, hid.at[pl.ds(at, ref.shape[0]), :]))
        at += ref.shape[0]
    pairs += list(zip(w_refs, w_bufs))
    copies = [pltpu.make_async_copy(a, b, sem.at[i]) for i, (a, b) in enumerate(pairs)]
    for c in copies:
        c.start()
    for c in copies[:n]:
        c.wait()
    starts = []
    first = 0
    for e in e_bufs:
        starts.append(first)
        first += e.shape[1]
    for k in (0, 2, 1):
        up, down, e = w_bufs[2 * k], w_bufs[2 * k + 1], e_bufs[k]
        width = e.shape[1]
        normed[:, pl.ds(0, width)] = layer_norm(hid[:, pl.ds(starts[k], width)]).astype(BF)
        copies[n + 2 * k].wait()
        hidden = [gelu(dot(normed[pl.ds(r, half), pl.ds(0, width)], up[...])).astype(BF) for r in (0, half)]
        copies[n + 2 * k + 1].wait()
        for i, r in enumerate((0, half)):
            e[pl.ds(r, half), :] = -dot(hidden[i], down[...])
        for b in range(0, width, BLK):

            @pl.when(me == (starts[k] + b) // slice_w)
            def _(b=b, e=e, k=k):
                e[:, pl.ds(b, BLK)] -= hid[:, pl.ds(starts[k] + b, BLK)].astype(F32)


def ffn(pieces, weights, slice_w, after):
    frames = sum(p.shape[0] for p in pieces)
    wall = pieces[0].shape[1]
    widths = [w.shape[1] for w in weights[1::2]]
    n = len(pieces)
    return call(
        functools.partial(ffn_kernel, slice_w, n),
        "ffn",
        [shape((frames, w), F32) for w in widths],
        [HBM] * (n + 6) + [ANY] * len(after),
        scratch=[pltpu.VMEM((frames, wall), BF)]
        + [pltpu.VMEM(w.shape, BF) for w in weights]
        + [pltpu.VMEM((frames, max(widths)), BF), pltpu.SemaphoreType.DMA((n + 6,))],
        limit=FFN_MB,
        us=13,
    )(*pieces, *weights, *after)


def student_kernel(dims, *refs):
    n_t, n_z, rows, out_rows = dims
    s_ref, w_refs, h_refs, refs = refs[0], refs[1 : 1 + 2 * n_z], refs[1 + 2 * n_z : 1 + 2 * n_z + 2 * n_t], refs[-19:]
    e_hbm, (h_keep, h_send, keep, send) = refs[:3], refs[3:7]
    w_in, w_out, w_head, pred, act, slope, err, student_t, *e_refs, sem = refs[7:]
    me_t = lax.axis_index("teacher")
    me_d = lax.axis_index("dp")
    z, core = me_d // 2, me_d % 2
    sd, sff = w_in.shape
    slice_w = w_head.shape[1] // n_t
    half_w = slice_w // 2
    parts = out_rows // rows
    pairs = []
    for i in range(2 * n_z):
        shard = 2 * lax.rem(z + n_z - i // 2, n_z) + (core if i % 2 == 0 else 1 - core)
        src = w_refs[i]
        pairs.append((src.at[:, pl.ds(0, sff)], w_in.at[aligned(shard, rows, 16), :]))
        for p in range(parts):
            at = pl.multiple_of(shard * out_rows + p * rows, 16)
            pairs.append((src.at[:, pl.ds(sff + p * sd, sd)], w_out.at[pl.ds(at, rows), :]))
    first = len(pairs)
    for k in range(n_t):
        for c in range(2):
            at = (me_t ^ k) * slice_w + (core if c == 0 else 1 - core) * half_w
            pairs.append((h_refs[2 * k + c], w_head.at[:, pl.ds(pl.multiple_of(at, 128), half_w)]))
    pairs += list(zip(e_hbm, e_refs))
    copies = [pltpu.make_async_copy(a, b, sem.at[i]) for i, (a, b) in enumerate(pairs)]
    for c in copies:
        c.start()
    order = [me_t ^ k for k in range(n_t)]
    student = jnp.concatenate([s_ref[k, :, pl.ds(0, sd)] for k in order], axis=0)
    mask = jnp.concatenate([s_ref[k, :, pl.ds(sd, 128)] for k in order], axis=0).astype(F32)
    student_t[...] = student.T
    for c in copies[:first]:
        c.wait()
    total = student.astype(F32)
    for b in range(0, sff, BLK):
        pre = dot(student, w_in[:, pl.ds(b, BLK)])
        low = pre - 4.0
        small = jnp.exp(-jnp.abs(low))
        swoosh = jnp.maximum(low, 0.0) + jnp.log(1.0 + small) - 0.08 * pre - 0.035
        swoosh = swoosh.astype(BF)
        act[:, pl.ds(b, BLK)] = swoosh
        slope[:, pl.ds(b, BLK)] = jnp.where(low >= 0.0, 1.0, small) / (1.0 + small) - 0.08
        total = total + dot(swoosh, w_out[pl.ds(b, BLK), :])
    features = total.astype(BF)
    feat_t = features.T
    for c in copies[first:]:
        c.wait()
    pred[...] = dot(features, w_head[:, aligned(me_t, slice_w, 128)])

    at = 0
    for ref in e_refs:
        width = ref.shape[1]
        scale = (2.0 / width) * mask
        for b in range(0, width, BLK):
            col = at + b
            value = ref[:, pl.ds(b, BLK)]
            guess = pred[:, pl.ds(col % slice_w, BLK)]
            value = value + jnp.where(me_t == col // slice_w, guess, 0.0)
            value = jnp.concatenate([value[:, c : c + 128] * scale for c in range(0, BLK, 128)], axis=1).astype(BF)
            err[:, pl.ds(col, BLK)] = value
            product = dot(feat_t, value)
            for i in range(n_z):
                low, high = product[2 * i * rows : (2 * i + 1) * rows], product[(2 * i + 1) * rows : 2 * (i + 1) * rows]
                h_keep[i, :, pl.ds(col, BLK)] = jnp.where(core == 0, low, high)
                h_send[i, :, pl.ds(col, BLK)] = jnp.where(core == 0, high, low).astype(BF)
        at += width

    fg = dot(err[...], w_head[...], ((1,), (1,))).astype(BF)
    block = sff // 4
    zs = block // (2 * out_rows)
    for b in range(4):
        part = dot(act[:, pl.ds(b * block, block)].T, fg)
        for i in range(zs):
            for p in range(parts):
                at = 2 * i * out_rows + p * rows
                low, high = part[at : at + rows], part[at + out_rows : at + out_rows + rows]
                lanes = pl.ds(p * sd, sd)
                keep[b * zs + i, :, lanes] = jnp.where(core == 0, low, high)
                send[b * zs + i, :, lanes] = jnp.where(core == 0, high, low).astype(BF)
        back = dot(fg, w_out[pl.ds(b * block, block), :], ((1,), (1,)))
        pre_grad = (back * slope[:, pl.ds(b * block, block)]).astype(BF)
        part = dot(student_t[...], pre_grad)
        for i in range(n_z):
            low, high = part[2 * i * rows : (2 * i + 1) * rows], part[(2 * i + 1) * rows : (2 * i + 2) * rows]
            lanes = pl.ds(parts * sd + b * block, block)
            keep[i, :, lanes] = jnp.where(core == 0, low, high)
            send[i, :, lanes] = jnp.where(core == 0, high, low).astype(BF)


def student_step(s_all, w_pieces, h_pieces, e_parts, n_z, rows, out_rows, sff):
    n_t, frames, sd = s_all.shape
    frames, sd = n_t * frames, sd - 128
    wall = sum(e.shape[1] for e in e_parts)
    wide = out_rows // rows * sd + sff
    return call(
        functools.partial(student_kernel, (n_t, n_z, rows, out_rows)),
        "student",
        [
            shape((n_z, rows, wall), F32),
            shape((n_z, rows, wall), BF),
            shape((n_z, rows, wide), F32),
            shape((n_z, rows, wide), BF),
        ],
        [VMEM] + [ANY] * (2 * n_z + 2 * n_t) + [HBM] * 3,
        scratch=[
            pltpu.VMEM((sd, sff), BF),
            pltpu.VMEM((sff, sd), BF),
            pltpu.VMEM((sd, wall), BF),
            pltpu.VMEM((frames, wall // n_t), F32),
            pltpu.VMEM((frames, sff), BF),
            pltpu.VMEM((frames, sff), F32),
            pltpu.VMEM((frames, wall), BF),
            pltpu.VMEM((sd, frames), BF),
        ]
        + [pltpu.VMEM(e.shape, F32) for e in e_parts]
        + [pltpu.SemaphoreType.DMA((2 * n_z * (1 + out_rows // rows) + 2 * n_t + 3,))],
        limit=STUDENT_MB,
        us=14,
    )(s_all, *w_pieces, *h_pieces, *e_parts)


def add_kernel(own, *refs):
    total = own[...]
    for r in refs[:-1]:
        total = total + r[...].astype(F32)
    refs[-1][...] = total.astype(refs[-1].dtype)


def chip_kernel(n_t, splits, keep, recv, *outs):
    me = lax.axis_index("teacher")
    own, sends = outs[0], outs[1:]
    at = 0
    for first, width in splits:
        w = width // n_t
        for k in range(n_t):
            t = me ^ k if len(sends) > 1 else k
            lanes = pl.ds(pl.multiple_of(first + t * w, 128), w)
            value = keep[:, :, lanes] + recv[:, :, lanes].astype(F32)
            if len(sends) > 1:
                dst = own if k == 0 else sends[k - 1]
                dst[:, :, pl.ds(at, w)] = value.astype(dst.dtype)
            else:
                sends[0][k, :, :, pl.ds(at, w)] = value.astype(BF)

                @pl.when(me == k)
                def _(value=value, at=at, w=w):
                    own[:, :, pl.ds(at, w)] = value

        at += w


def teacher_kernel(n_t, n_z, mine, *refs):
    got, own, sends = refs[: -n_z], refs[-n_z], refs[len(refs) - n_z + 1 :]
    z = lax.axis_index("dp") // 2
    me = lax.axis_index("teacher")
    for k in range(n_z):
        at = z ^ k
        total = mine[at]
        for j in range(1, n_t):
            value = got[0][me ^ j, at] if len(got) == 1 else got[j - 1][at]
            total = total + value.astype(F32)
        dst = own if k == 0 else sends[k - 1]
        dst[...] = total.astype(dst.dtype)


def last_kernel(n_t, *refs):
    heads, rest, (g_in, g_out, g_head) = refs[:n_t], refs[n_t : 2 * n_t], refs[2 * n_t :]
    me = lax.axis_index("teacher")
    rows = g_in.shape[0]
    parts = g_out.shape[0] // rows
    ow, iw, hw = g_out.shape[1] // n_t, g_in.shape[1] // n_t, g_head.shape[1] // n_t
    for k in range(n_t):
        at = me ^ k
        g_head[:, aligned(at, hw, 128)] = heads[k][...]
        for p in range(parts):
            g_out[pl.ds(p * rows, rows), aligned(at, ow, 128)] = rest[k][:, pl.ds(p * ow, ow)]
        g_in[:, aligned(at, iw, 128)] = rest[k][:, pl.ds(parts * ow, iw)]


def make_body(n_t, n_dp):
    n_z = n_dp // 2

    def swap_t(k, value):
        return lax.ppermute(value, "teacher", [(t, t ^ k) for t in range(n_t)])

    def shift_z(k, value):
        return lax.ppermute(value, "dp", [(d, (d + 2 * k) % n_dp) for d in range(n_dp)])

    def swap_z(k, value):
        return lax.ppermute(value, "dp", [(d, d ^ (2 * k)) for d in range(n_dp)])

    def swap_core(value):
        return lax.ppermute(value, "dp", [(d, d ^ 1) for d in range(n_dp)])

    def body(hid_whisper, hid_beats, hid_wavlm, up_whisper, down_whisper, up_beats, down_beats,
             up_wavlm, down_wavlm, clip_len, send_counts, student_in, w_in, w_out, w_head):
        frames, sd = student_in.shape
        half = frames // 2
        cap = 2 * frames // n_dp
        rows, sff = w_in.shape
        out_rows = w_out.shape[0]
        parts = out_rows // rows
        wall = w_head.shape[1]
        slice_w = wall // n_t
        packed = call(
            functools.partial(pack_kernel, n_t, n_dp, cap), "pack",
            shape((n_dp * rows, (sd + slice_w) // 2), BF), [SMEM, VMEM, VMEM], limit=60,
        )(send_counts, student_in, w_head)
        arrived = lax.all_to_all(packed, "dp", split_axis=0, concat_axis=0, tiled=True)

        merged, hid = call(
            merge_kernel, "merge", [shape((rows, sff + parts * sd), BF), shape((frames, wall), BF)],
            [HBM] * 5 + [ANY], scratch=[pltpu.SemaphoreType.DMA((parts + 4,))], limit=60,
        )(w_in, w_out, hid_whisper, hid_beats, hid_wavlm, packed)
        from_x, from_y = swap_t(1, hid), swap_t(2, hid)
        to_y, to_x = call(
            halves_kernel, "halves", [shape((half, wall), BF)] * 2, [HBM] * 2,
            scratch=[pltpu.SemaphoreType.DMA((2,))], limit=4,
        )(from_x, from_y)
        group = [hid, from_x, from_y, swap_t(1, to_x), swap_t(2, to_y)]
        from_z = [merged]
        for k in range(1, n_z):
            value = from_z[-1]
            if k == 2:
                value, *group = lax.optimization_barrier((value, *group))
            from_z.append(shift_z(1, value))

        s_own, head = call(
            functools.partial(unpack_kernel, n_dp, cap), "unpack",
            [shape((n_t, frames, sd + 128), BF), shape((sd, slice_w // 2), BF)], [SMEM, SMEM, VMEM], limit=8,
        )(send_counts, clip_len, arrived)
        s_all = lax.all_to_all(s_own, "teacher", split_axis=0, concat_axis=0, tiled=True)
        h_mine = [head] + [swap_t(k, head) for k in range(1, n_t)]
        e_parts = ffn(group, (up_whisper, down_whisper, up_beats, down_beats, up_wavlm, down_wavlm), slice_w, (s_own, from_z[-2]))
        from_z, h_mine, s_all, _ = lax.optimization_barrier((from_z, h_mine, s_all, e_parts[0]))
        w_pieces, h_pieces = [], []
        for piece in from_z:
            w_pieces += [piece, swap_core(piece)]
        for piece in h_mine:
            h_pieces += [piece, swap_core(piece)]

        h_keep, h_send, keep, send = student_step(s_all, w_pieces, h_pieces, e_parts, n_z, rows, out_rows, sff)

        def chip_sum(keep, send, splits, many):
            chunk = keep.shape[2] // n_t
            sends = [shape((n_z, rows, chunk), BF)] * (n_t - 1) if many else [shape((n_t, n_z, rows, chunk), BF)]
            return call(
                functools.partial(chip_kernel, n_t, splits), "chip",
                [shape((n_z, rows, chunk), F32)] + sends, [VMEM] * 2,
            )(keep, swap_core(send))

        def z_sum(mine, got):
            chunk = mine.shape[2]
            own, *sends = call(
                functools.partial(teacher_kernel, n_t, n_z), "over_teacher",
                [shape((rows, chunk), F32)] + [shape((rows, chunk), BF)] * (n_z - 1), [VMEM] * (1 + len(got)),
            )(mine, *got)
            got = [swap_z(k + 1, v) for k, v in enumerate(sends)]
            total = call(add_kernel, "over_z", shape((rows, chunk), F32), [VMEM] * n_z)(own, *got)
            return [total] + [swap_t(k, total) for k in range(1, n_t)]

        h_own, *h_sends = chip_sum(h_keep, h_send, [(0, wall)], True)
        h_got = [swap_t(k + 1, v) for k, v in enumerate(h_sends)]
        splits = [(p * sd, sd) for p in range(parts)] + [(parts * sd, sff)]
        r_own, *r_sends = chip_sum(keep, send, splits, True)
        r_got = [swap_t(k + 1, v) for k, v in enumerate(r_sends)]
        h_all = z_sum(h_own, h_got)
        r_all = z_sum(r_own, r_got)
        grad_in, grad_out, grad_head = call(
            functools.partial(last_kernel, n_t), "last",
            [shape((rows, sff), F32), shape((out_rows, sd), F32), shape((rows, wall), F32)], [VMEM] * (2 * n_t),
        )(*h_all, *r_all)
        return grad_in, grad_out, grad_head

    return body


def solution(mesh):
    rows = P(("teacher", "dp"), None)
    in_specs = (
        rows, rows, rows,
        P(None, "teacher"), P("teacher", None),
        P(None, "teacher"), P("teacher", None),
        P(None, "teacher"), P("teacher", None),
        P(("teacher", "dp")), P("teacher", None, None), rows,
        P("dp", None), P("dp", None), P("dp", None),
    )
    out_specs = (P("dp", None), P("dp", None), P("dp", None))
    body = make_body(mesh.shape["teacher"], mesh.shape["dp"])
    return jax.shard_map(body, mesh=mesh, in_specs=in_specs, out_specs=out_specs, check_vma=False)
```

```python
import functools

import jax
import jax.numpy as jnp
from jax import lax
from jax.experimental import pallas as pl
from jax.experimental.pallas import tpu as pltpu
from jax.sharding import PartitionSpec as P

EPS = 1e-05
BF = jnp.bfloat16
F32 = jnp.float32
I32 = jnp.int32
BLK = 256
FFN_MB = 57
STUDENT_MB = 44
VMEM = pl.BlockSpec(memory_space=pltpu.VMEM)
SMEM = pl.BlockSpec(memory_space=pltpu.SMEM)
ANY = pl.BlockSpec(memory_space=pl.ANY)
HBM = pl.BlockSpec(memory_space=pltpu.HBM)


def dot(a, b, dims=((1,), (0,))):
    return lax.dot_general(a, b, (dims, ((), ())), preferred_element_type=F32)


def layer_norm(values):
    wide = values.astype(F32)
    center = wide - jnp.mean(wide, axis=-1, keepdims=True)
    spread = jnp.mean(center * center, axis=-1, keepdims=True)
    return center * lax.rsqrt(spread + EPS)


def gelu(x):
    return 0.5 * x * (1.0 + lax.erf(x * 0.7071067811865476))


def aligned(index, size, to):
    return pl.ds(pl.multiple_of(index * size, to), size)


def call(kernel, name, out_shape, in_specs, scratch=(), out_specs=None, limit=8, us=1):
    many = isinstance(out_shape, (list, tuple))
    if out_specs is None:
        out_specs = [VMEM] * len(out_shape) if many else VMEM
    return pl.pallas_call(
        kernel,
        out_shape=out_shape,
        in_specs=in_specs,
        out_specs=out_specs,
        scratch_shapes=list(scratch),
        name=name,
        cost_estimate=pl.CostEstimate(flops=int(us * 1e9), bytes_accessed=int(us * 3e6), transcendentals=0),
        compiler_params=pltpu.CompilerParams(vmem_limit_bytes=limit * 1024 * 1024),
    )


def shape(dims, dtype):
    return jax.ShapeDtypeStruct(dims, dtype)


def pack_kernel(n_t, n_dp, cap, table, student, w_head, out):
    me = lax.axis_index("dp")
    frames, sd = student.shape
    rows = 2 * cap
    row = lax.broadcasted_iota(I32, (n_dp * rows, frames), 0)
    col = lax.broadcasted_iota(I32, (n_dp * rows, frames), 1)
    start = jnp.zeros((n_dp * rows, frames), I32)
    running = jnp.int32(0)
    for s in range(n_dp):
        start = jnp.where(row // rows == s, running, start)
        running = running + table[0, s, me]
    pick = (col == start + row % cap).astype(F32).astype(BF)
    half = sd // 2
    left, right = dot(pick, student[:, :half]), dot(pick, student[:, half:])
    first = lax.broadcasted_iota(I32, left.shape, 0) % rows < cap
    out[:, :half] = jnp.where(first, left, right).astype(BF)
    slice_w = w_head.shape[1] // n_t
    mine = w_head[:, aligned(lax.axis_index("teacher"), slice_w, 128)]
    for d in range(n_dp):
        lane = d % 2 * (slice_w // 2)
        out[pl.ds(d * rows, rows), half:] = mine[:, lane : lane + slice_w // 2]


def unpack_kernel(n_dp, cap, table, clip_len, arrived, out, head):
    me = lax.axis_index("dp")
    copies, frames, wide = out.shape
    sd = wide - 128
    half = sd // 2
    rows = 2 * cap
    row = lax.broadcasted_iota(I32, (frames, n_dp * rows), 0)
    col = lax.broadcasted_iota(I32, (frames, n_dp * rows), 1)
    slot = jnp.zeros((frames, n_dp * rows), I32)
    running = jnp.int32(0)
    for o in range(n_dp):
        here = table[0, me, o]
        inside = (row >= running) & (row < running + here)
        slot = jnp.where(inside, o * rows + row - running, slot)
        running = running + here
    parts = [
        dot((col == slot + at).astype(F32).astype(BF), arrived[:, :half]).astype(BF) for at in (0, cap)
    ]
    clips = clip_len.shape[0]
    slots = frames // clips
    frame = lax.broadcasted_iota(I32, (frames, wide - sd), 0)
    valid = jnp.zeros((frames, wide - sd), F32)
    for c in range(clips):
        used = (frame // slots == c) & (frame % slots < clip_len[c])
        valid = jnp.where(used, 1.0, valid)
    for k in range(copies):
        out[k, :, :half] = parts[0]
        out[k, :, half:sd] = parts[1]
        out[k, :, sd:] = valid.astype(BF)
    head[...] = arrived[:, half:]


def copy_all(pairs, sem):
    copies = [pltpu.make_async_copy(a, b, sem.at[i]) for i, (a, b) in enumerate(pairs)]
    for c in copies:
        c.start()
    for c in copies:
        c.wait()


def merge_kernel(w_in, w_out, whisper, beats, wavlm, after, merged, hid, sem):
    rows, sff = w_in.shape
    sd = w_out.shape[1]
    pairs = [(w_in, merged.at[:, pl.ds(0, sff)])]
    for p in range(w_out.shape[0] // rows):
        pairs.append((w_out.at[pl.ds(p * rows, rows), :], merged.at[:, pl.ds(sff + p * sd, sd)]))
    at = 0
    for ref in (whisper, beats, wavlm):
        pairs.append((ref, hid.at[:, pl.ds(at, ref.shape[1])]))
        at += ref.shape[1]
    copy_all(pairs, sem)


def halves_kernel(from_x, from_y, *refs):
    to_y, to_x, sem = refs[-3:]
    half = to_x.shape[0]
    copy_all([(from_x.at[pl.ds(half, half), :], to_y), (from_y.at[pl.ds(0, half), :], to_x)], sem)


def ffn_kernel(slice_w, n, *refs):
    h_refs, w_refs, refs = refs[:n], refs[n : n + 6], refs[-12:]
    e_bufs, hid, w_bufs, (normed, sem) = refs[:3], refs[3], refs[4:10], refs[10:]
    me = lax.axis_index("teacher")
    frames = hid.shape[0]
    half = frames // 2
    pairs = []
    at = 0
    for ref in h_refs:
        pairs.append((ref, hid.at[pl.ds(at, ref.shape[0]), :]))
        at += ref.shape[0]
    pairs += list(zip(w_refs, w_bufs))
    copies = [pltpu.make_async_copy(a, b, sem.at[i]) for i, (a, b) in enumerate(pairs)]
    for i in [*range(n), n + 2, n + 3, n + 4, n + 5, n, n + 1]:
        copies[i].start()
    for c in copies[:n]:
        c.wait()
    starts = []
    first = 0
    for e in e_bufs:
        starts.append(first)
        first += e.shape[1]
    for k in (1, 2, 0):
        up, down, e = w_bufs[2 * k], w_bufs[2 * k + 1], e_bufs[k]
        width = e.shape[1]
        normed[:, pl.ds(0, width)] = layer_norm(hid[:, pl.ds(starts[k], width)]).astype(BF)
        copies[n + 2 * k].wait()
        hidden = [gelu(dot(normed[pl.ds(r, half), pl.ds(0, width)], up[...])).astype(BF) for r in (0, half)]
        copies[n + 2 * k + 1].wait()
        for i, r in enumerate((0, half)):
            e[pl.ds(r, half), :] = -dot(hidden[i], down[...])
        for b in range(0, width, BLK):

            @pl.when(me == (starts[k] + b) // slice_w)
            def _(b=b, e=e, k=k):
                e[:, pl.ds(b, BLK)] -= hid[:, pl.ds(starts[k] + b, BLK)].astype(F32)


def ffn(pieces, weights, slice_w, after):
    frames = sum(p.shape[0] for p in pieces)
    wall = pieces[0].shape[1]
    widths = [w.shape[1] for w in weights[1::2]]
    n = len(pieces)
    return call(
        functools.partial(ffn_kernel, slice_w, n),
        "ffn",
        [shape((frames, w), F32) for w in widths],
        [HBM] * (n + 6) + [ANY] * len(after),
        scratch=[pltpu.VMEM((frames, wall), BF)]
        + [pltpu.VMEM(w.shape, BF) for w in weights]
        + [pltpu.VMEM((frames, max(widths)), BF), pltpu.SemaphoreType.DMA((n + 6,))],
        limit=FFN_MB,
        us=13,
    )(*pieces, *weights, *after)


def student_kernel(dims, *refs):
    n_t, n_z, rows, out_rows = dims
    s_ref, w_refs, h_refs, refs = refs[0], refs[1 : 1 + 2 * n_z], refs[1 + 2 * n_z : 1 + 2 * n_z + 2 * n_t], refs[-19:]
    e_hbm, (h_keep, h_send, keep, send) = refs[:3], refs[3:7]
    w_in, w_out, w_head, pred, act, slope, err, student_t, *e_refs, sem = refs[7:]
    me_t = lax.axis_index("teacher")
    me_d = lax.axis_index("dp")
    z, core = me_d // 2, me_d % 2
    sd, sff = w_in.shape
    slice_w = w_head.shape[1] // n_t
    half_w = slice_w // 2
    parts = out_rows // rows
    pairs = []
    for i in range(2 * n_z):
        shard = 2 * lax.rem(z + n_z - i // 2, n_z) + (core if i % 2 == 0 else 1 - core)
        src = w_refs[i]
        pairs.append((src.at[:, pl.ds(0, sff)], w_in.at[aligned(shard, rows, 16), :]))
        for p in range(parts):
            at = pl.multiple_of(shard * out_rows + p * rows, 16)
            pairs.append((src.at[:, pl.ds(sff + p * sd, sd)], w_out.at[pl.ds(at, rows), :]))
    first = len(pairs)
    for k in range(n_t):
        for c in range(2):
            at = (me_t ^ k) * slice_w + (core if c == 0 else 1 - core) * half_w
            pairs.append((h_refs[2 * k + c], w_head.at[:, pl.ds(pl.multiple_of(at, 128), half_w)]))
    pairs += list(zip(e_hbm, e_refs))
    copies = [pltpu.make_async_copy(a, b, sem.at[i]) for i, (a, b) in enumerate(pairs)]
    for c in copies:
        c.start()
    order = [me_t ^ k for k in range(n_t)]
    student = jnp.concatenate([s_ref[k, :, pl.ds(0, sd)] for k in order], axis=0)
    mask = jnp.concatenate([s_ref[k, :, pl.ds(sd, 128)] for k in order], axis=0).astype(F32)
    student_t[...] = student.T
    for c in copies[:first]:
        c.wait()
    total = student.astype(F32)
    for b in range(0, sff, BLK):
        pre = dot(student, w_in[:, pl.ds(b, BLK)])
        low = pre - 4.0
        small = jnp.exp(-jnp.abs(low))
        swoosh = jnp.maximum(low, 0.0) + jnp.log(1.0 + small) - 0.08 * pre - 0.035
        swoosh = swoosh.astype(BF)
        act[:, pl.ds(b, BLK)] = swoosh
        slope[:, pl.ds(b, BLK)] = jnp.where(low >= 0.0, 1.0, small) / (1.0 + small) - 0.08
        total = total + dot(swoosh, w_out[pl.ds(b, BLK), :])
    features = total.astype(BF)
    feat_t = features.T
    for c in copies[first:]:
        c.wait()
    pred[...] = dot(features, w_head[:, aligned(me_t, slice_w, 128)])

    at = 0
    for ref in e_refs:
        width = ref.shape[1]
        scale = (2.0 / width) * mask
        for b in range(0, width, BLK):
            col = at + b
            value = ref[:, pl.ds(b, BLK)]
            guess = pred[:, pl.ds(col % slice_w, BLK)]
            value = value + jnp.where(me_t == col // slice_w, guess, 0.0)
            value = jnp.concatenate([value[:, c : c + 128] * scale for c in range(0, BLK, 128)], axis=1).astype(BF)
            err[:, pl.ds(col, BLK)] = value
            product = dot(feat_t, value)
            for i in range(n_z):
                low, high = product[2 * i * rows : (2 * i + 1) * rows], product[(2 * i + 1) * rows : 2 * (i + 1) * rows]
                h_keep[i, :, pl.ds(col, BLK)] = jnp.where(core == 0, low, high)
                h_send[i, :, pl.ds(col, BLK)] = jnp.where(core == 0, high, low).astype(BF)
        at += width

    fg = dot(err[...], w_head[...], ((1,), (1,))).astype(BF)
    block = sff // 4
    zs = block // (2 * out_rows)
    for b in range(4):
        part = dot(act[:, pl.ds(b * block, block)].T, fg)
        for i in range(zs):
            for p in range(parts):
                at = 2 * i * out_rows + p * rows
                low, high = part[at : at + rows], part[at + out_rows : at + out_rows + rows]
                lanes = pl.ds(p * sd, sd)
                keep[b * zs + i, :, lanes] = jnp.where(core == 0, low, high)
                send[b * zs + i, :, lanes] = jnp.where(core == 0, high, low).astype(BF)
        back = dot(fg, w_out[pl.ds(b * block, block), :], ((1,), (1,)))
        pre_grad = (back * slope[:, pl.ds(b * block, block)]).astype(BF)
        part = dot(student_t[...], pre_grad)
        for i in range(n_z):
            low, high = part[2 * i * rows : (2 * i + 1) * rows], part[(2 * i + 1) * rows : (2 * i + 2) * rows]
            lanes = pl.ds(parts * sd + b * block, block)
            keep[i, :, lanes] = jnp.where(core == 0, low, high)
            send[i, :, lanes] = jnp.where(core == 0, high, low).astype(BF)


def student_step(s_all, w_pieces, h_pieces, e_parts, n_z, rows, out_rows, sff):
    n_t, frames, sd = s_all.shape
    frames, sd = n_t * frames, sd - 128
    wall = sum(e.shape[1] for e in e_parts)
    wide = out_rows // rows * sd + sff
    return call(
        functools.partial(student_kernel, (n_t, n_z, rows, out_rows)),
        "student",
        [
            shape((n_z, rows, wall), F32),
            shape((n_z, rows, wall), BF),
            shape((n_z, rows, wide), F32),
            shape((n_z, rows, wide), BF),
        ],
        [VMEM] + [ANY] * (2 * n_z + 2 * n_t) + [HBM] * 3,
        scratch=[
            pltpu.VMEM((sd, sff), BF),
            pltpu.VMEM((sff, sd), BF),
            pltpu.VMEM((sd, wall), BF),
            pltpu.VMEM((frames, wall // n_t), F32),
            pltpu.VMEM((frames, sff), BF),
            pltpu.VMEM((frames, sff), F32),
            pltpu.VMEM((frames, wall), BF),
            pltpu.VMEM((sd, frames), BF),
        ]
        + [pltpu.VMEM(e.shape, F32) for e in e_parts]
        + [pltpu.SemaphoreType.DMA((2 * n_z * (1 + out_rows // rows) + 2 * n_t + 3,))],
        limit=STUDENT_MB,
        us=14,
    )(s_all, *w_pieces, *h_pieces, *e_parts)


def add_kernel(own, *refs):
    total = own[...]
    for r in refs[:-1]:
        total = total + r[...].astype(F32)
    refs[-1][...] = total.astype(refs[-1].dtype)


def chip_kernel(n_t, splits, keep, recv, *outs):
    me = lax.axis_index("teacher")
    own, sends = outs[0], outs[1:]
    at = 0
    for first, width in splits:
        w = width // n_t
        for k in range(n_t):
            t = me ^ k if len(sends) > 1 else k
            lanes = pl.ds(pl.multiple_of(first + t * w, 128), w)
            value = keep[:, :, lanes] + recv[:, :, lanes].astype(F32)
            if len(sends) > 1:
                dst = own if k == 0 else sends[k - 1]
                dst[:, :, pl.ds(at, w)] = value.astype(dst.dtype)
            else:
                sends[0][k, :, :, pl.ds(at, w)] = value.astype(BF)

                @pl.when(me == k)
                def _(value=value, at=at, w=w):
                    own[:, :, pl.ds(at, w)] = value

        at += w


def teacher_kernel(n_t, n_z, mine, *refs):
    got, own, sends = refs[: -n_z], refs[-n_z], refs[len(refs) - n_z + 1 :]
    z = lax.axis_index("dp") // 2
    me = lax.axis_index("teacher")
    for k in range(n_z):
        at = z ^ k
        total = mine[at]
        for j in range(1, n_t):
            value = got[0][me ^ j, at] if len(got) == 1 else got[j - 1][at]
            total = total + value.astype(F32)
        dst = own if k == 0 else sends[k - 1]
        dst[...] = total.astype(dst.dtype)


def last_kernel(n_t, *refs):
    heads, rest, (g_in, g_out, g_head) = refs[:n_t], refs[n_t : 2 * n_t], refs[2 * n_t :]
    me = lax.axis_index("teacher")
    rows = g_in.shape[0]
    parts = g_out.shape[0] // rows
    ow, iw, hw = g_out.shape[1] // n_t, g_in.shape[1] // n_t, g_head.shape[1] // n_t
    for k in range(n_t):
        at = me ^ k
        g_head[:, aligned(at, hw, 128)] = heads[k][...]
        for p in range(parts):
            g_out[pl.ds(p * rows, rows), aligned(at, ow, 128)] = rest[k][:, pl.ds(p * ow, ow)]
        g_in[:, aligned(at, iw, 128)] = rest[k][:, pl.ds(parts * ow, iw)]


def make_body(n_t, n_dp):
    n_z = n_dp // 2

    def swap_t(k, value):
        return lax.ppermute(value, "teacher", [(t, t ^ k) for t in range(n_t)])

    def shift_z(k, value):
        return lax.ppermute(value, "dp", [(d, (d + 2 * k) % n_dp) for d in range(n_dp)])

    def swap_z(k, value):
        return lax.ppermute(value, "dp", [(d, d ^ (2 * k)) for d in range(n_dp)])

    def swap_core(value):
        return lax.ppermute(value, "dp", [(d, d ^ 1) for d in range(n_dp)])

    def body(hid_whisper, hid_beats, hid_wavlm, up_whisper, down_whisper, up_beats, down_beats,
             up_wavlm, down_wavlm, clip_len, send_counts, student_in, w_in, w_out, w_head):
        frames, sd = student_in.shape
        half = frames // 2
        cap = 2 * frames // n_dp
        rows, sff = w_in.shape
        out_rows = w_out.shape[0]
        parts = out_rows // rows
        wall = w_head.shape[1]
        slice_w = wall // n_t
        packed = call(
            functools.partial(pack_kernel, n_t, n_dp, cap), "pack",
            shape((n_dp * rows, (sd + slice_w) // 2), BF), [SMEM, VMEM, VMEM], limit=60,
        )(send_counts, student_in, w_head)
        arrived = lax.all_to_all(packed, "dp", split_axis=0, concat_axis=0, tiled=True)

        merged, hid = call(
            merge_kernel, "merge", [shape((rows, sff + parts * sd), BF), shape((frames, wall), BF)],
            [HBM] * 5 + [ANY], scratch=[pltpu.SemaphoreType.DMA((parts + 4,))], limit=60,
        )(w_in, w_out, hid_whisper, hid_beats, hid_wavlm, packed)
        from_x, from_y = swap_t(1, hid), swap_t(2, hid)
        to_y, to_x = call(
            halves_kernel, "halves", [shape((half, wall), BF)] * 2, [HBM] * 2,
            scratch=[pltpu.SemaphoreType.DMA((2,))], limit=4,
        )(from_x, from_y)
        group = [hid, from_x, from_y, swap_t(1, to_x), swap_t(2, to_y)]
        from_z = [merged]
        for k in range(1, n_z):
            value = from_z[-1]
            if k == 2:
                value, *group = lax.optimization_barrier((value, *group))
            from_z.append(shift_z(1, value))

        s_own, head = call(
            functools.partial(unpack_kernel, n_dp, cap), "unpack",
            [shape((n_t, frames, sd + 128), BF), shape((sd, slice_w // 2), BF)], [SMEM, SMEM, VMEM], limit=8,
        )(send_counts, clip_len, arrived)
        s_all = lax.all_to_all(s_own, "teacher", split_axis=0, concat_axis=0, tiled=True)
        h_mine = [head] + [swap_t(k, head) for k in range(1, n_t)]
        e_parts = ffn(group, (up_whisper, down_whisper, up_beats, down_beats, up_wavlm, down_wavlm), slice_w, (s_own, from_z[-2]))
        from_z, h_mine, s_all, _ = lax.optimization_barrier((from_z, h_mine, s_all, e_parts[0]))
        w_pieces, h_pieces = [], []
        for piece in from_z:
            w_pieces += [piece, swap_core(piece)]
        for piece in h_mine:
            h_pieces += [piece, swap_core(piece)]

        h_keep, h_send, keep, send = student_step(s_all, w_pieces, h_pieces, e_parts, n_z, rows, out_rows, sff)

        def chip_sum(keep, send, splits, many):
            chunk = keep.shape[2] // n_t
            sends = [shape((n_z, rows, chunk), BF)] * (n_t - 1) if many else [shape((n_t, n_z, rows, chunk), BF)]
            return call(
                functools.partial(chip_kernel, n_t, splits), "chip",
                [shape((n_z, rows, chunk), F32)] + sends, [VMEM] * 2,
            )(keep, swap_core(send))

        def z_sum(mine, got):
            chunk = mine.shape[2]
            own, *sends = call(
                functools.partial(teacher_kernel, n_t, n_z), "over_teacher",
                [shape((rows, chunk), F32)] + [shape((rows, chunk), BF)] * (n_z - 1), [VMEM] * (1 + len(got)),
            )(mine, *got)
            got = [swap_z(k + 1, v) for k, v in enumerate(sends)]
            total = call(add_kernel, "over_z", shape((rows, chunk), F32), [VMEM] * n_z)(own, *got)
            return [total] + [swap_t(k, total) for k in range(1, n_t)]

        h_own, *h_sends = chip_sum(h_keep, h_send, [(0, wall)], True)
        h_got = [swap_t(k + 1, v) for k, v in enumerate(h_sends)]
        splits = [(p * sd, sd) for p in range(parts)] + [(parts * sd, sff)]
        r_own, *r_sends = chip_sum(keep, send, splits, True)
        r_got = [swap_t(k + 1, v) for k, v in enumerate(r_sends)]
        h_all = z_sum(h_own, h_got)
        r_all = z_sum(r_own, r_got)
        grad_in, grad_out, grad_head = call(
            functools.partial(last_kernel, n_t), "last",
            [shape((rows, sff), F32), shape((out_rows, sd), F32), shape((rows, wall), F32)], [VMEM] * (2 * n_t),
        )(*h_all, *r_all)
        return grad_in, grad_out, grad_head

    return body


def solution(mesh):
    rows = P(("teacher", "dp"), None)
    in_specs = (
        rows, rows, rows,
        P(None, "teacher"), P("teacher", None),
        P(None, "teacher"), P("teacher", None),
        P(None, "teacher"), P("teacher", None),
        P(("teacher", "dp")), P("teacher", None, None), rows,
        P("dp", None), P("dp", None), P("dp", None),
    )
    out_specs = (P("dp", None), P("dp", None), P("dp", None))
    body = make_body(mesh.shape["teacher"], mesh.shape["dp"])
    return jax.shard_map(body, mesh=mesh, in_specs=in_specs, out_specs=out_specs, check_vma=False)
```
